512 devices in a mesh: section: 16 (over z), seq: 32 (over x, y, core).
Axes of the slice: x: 4, y: 4, z: 16, core: 2. Of those that a mesh axis runs over, the one named last changes fastest.
Arguments:
- section_input: bfloat16 [16, 4096, 4096], P('section', 'seq'), may hold values from -30 to 30
- cotangent: bfloat16 [16, 4096, 4096], P('section', 'seq'), may hold values from -6 to 6
- norm_gain: float32 [16, 4096], P('section'), may hold values from 0.1 to 1.9
- short_filter: float32 [16, 3, 3, 4096], P('section'), may hold values from -3.5 to 3.5
- decay_rate: float32 [16, 16, 4096], P('section'), may hold values from 4.8828124e-06 to 0.06
- residue: float32 [16, 16, 4096], P('section'), may hold values from -1.5 to 1.5
- skip_gain: float32 [16, 4096], P('section'), may hold values from 0.5 to 1.5
Outputs:
- passed_on: bfloat16 [16, 4096, 4096], P('section', 'seq')
- passed_back: bfloat16 [16, 4096, 4096], P('section', 'seq')
The draws below stay inside these ranges and needn't reach their ends.
All inputs are finite; a program needn't handle non-finite values.
Results may differ from the reference program's by a relative error of at most 0.005.
Values may be sent and summed in bfloat16 or wider, within the bound.
No kernel may reach another device: no remote copies, remote signals or barrier semaphores. Data moves between devices by JAX's collectives and lax.ppermute only.
A program may use at most 192 MiB of HBM per device.

```python
import math
import jax
import jax.numpy as jnp
from jax import lax

WIDTH = 4096
MODES = 16
TAPS = 3
SECTIONS = 16
SEQ_LEN = 4096


def draw_section_input(key, part):
    key = jax.random.fold_in(key, 11)
    row_key, col_key, base_key = jax.random.split(key, 3)
    shape = (SECTIONS, SEQ_LEN, WIDTH)
    row_scale = jnp.exp(jax.random.uniform(row_key, (SECTIONS, SEQ_LEN, 1), jnp.float32, -1.15, 1.15))
    col_scale = jnp.exp(jax.random.uniform(col_key, (SECTIONS, 1, WIDTH), jnp.float32, -1.15, 1.15))
    base = jnp.clip(jax.random.normal(base_key, shape, jnp.float32), -3.0, 3.0)
    return (base * row_scale * col_scale).astype(jnp.bfloat16)


def level_of(stream_key, shape, pieces, smallest, high):
    factor_of, own = 1.0, jax.random.fold_in(stream_key, 6)
    for dim, shards_of in pieces:
        steps = jnp.exp(jax.random.uniform(jax.random.fold_in(own, dim), (shards_of,), jnp.float32, smallest / len(pieces), high / len(pieces)))
        factor_of = factor_of * jnp.repeat(steps, shape[dim] // shards_of).reshape([-1 if axis == dim else 1 for axis in range(len(shape))])
    return factor_of


def scatter_about(key, shape, scale, reach, cuts=(), kind=jnp.bfloat16):
    values = jax.random.normal(key, shape, jnp.float32) * scale
    if len(cuts) > 0:
        values = level_of(key, shape, cuts, -0.22, 0.18) * values
    return jnp.clip(values, min=-reach, max=reach).astype(kind)


def setup_inputs(seed: int = 0) -> dict:
    splits = jax.random.split(jax.random.key(seed), 8)
    section_input = draw_section_input(jax.random.fold_in(splits[7], 71), 0)
    cotangent = scatter_about(splits[1], (SECTIONS, SEQ_LEN, WIDTH), 1.0, 6.0, ((0, 16), (1, 32)))
    norm_gain = jnp.clip(1.0 + 0.18 * jax.random.normal(splits[2], (SECTIONS, WIDTH), jnp.float32), 0.1, 1.9)
    short_filter = scatter_about(splits[3], (SECTIONS, 3, TAPS, WIDTH), TAPS ** -0.5, 3.5, ((0, 16),), jnp.float32)
    decay_rate = jnp.clip(jnp.exp(math.log(0.06) - 9.416378 * jax.random.uniform(splits[4], (SECTIONS, MODES, WIDTH), jnp.float32) ** level_of(splits[4], (SECTIONS, MODES, WIDTH), ((0, 16),), -0.2, 0.2)), 4.882812390860636e-06, 0.06)
    residue = scatter_about(splits[5], (SECTIONS, MODES, WIDTH), MODES ** -0.5, 1.5, ((0, 16),), jnp.float32)
    skip_gain = jnp.clip(0.5 + 1.0 * jax.random.uniform(splits[6], (SECTIONS, WIDTH), jnp.float32) ** level_of(splits[6], (SECTIONS, WIDTH), ((0, 16),), -0.2, 0.2), 0.5, 1.5)
    return {"section_input": section_input, "cotangent": cotangent, "norm_gain": norm_gain, "short_filter": short_filter, "decay_rate": decay_rate, "residue": residue, "skip_gain": skip_gain}


def filter_taps(rates, coefs, length):
    steps = jnp.arange(length).astype(jnp.float32)

    def add_mode(index, total):
        return total + coefs[index][None, :] * jnp.exp(-rates[index][None, :] * steps[:, None])
    return lax.fori_loop(0, MODES, add_mode, jnp.zeros((length, rates.shape[1]), jnp.float32))

def causal_apply(taps, signal):
    length = signal.shape[0]
    spectrum = jnp.fft.rfft(taps, n=2 * length, axis=0) * jnp.fft.rfft(signal, n=2 * length, axis=0)
    return jnp.fft.irfft(spectrum, n=2 * length, axis=0)[:length]

def delayed(field, lag):
    return jnp.pad(field, ((lag, 0), (0, 0)))[:field.shape[0]]

def advanced(field, lag):
    return jnp.pad(field, ((0, lag), (0, 0)))[lag:]

def one_section(inputs):
    section_input, cotangent, gain, taps, rates, residue, skip = inputs
    x_rows = section_input.astype(jnp.float32)
    grad_out = cotangent.astype(jnp.float32)
    inverse = lax.rsqrt(lax.optimization_barrier(jnp.mean(x_rows * x_rows, axis=-1, keepdims=True)) + 1e-06)
    normed = x_rows * inverse * gain
    branches = []
    for branch in range(3):
        total = jnp.zeros_like(normed)
        for lag in range(TAPS):
            total = total + taps[branch, lag] * delayed(normed, lag)
        branches.append(total)
    query_rows, key_rows, value_rows = branches
    mixed_in = (key_rows * value_rows).astype(jnp.bfloat16)
    gate_grad = (grad_out * query_rows).astype(jnp.bfloat16)
    coefs = residue * jnp.sqrt(1.0 - jnp.exp(-2.0 * rates))
    long_filter = filter_taps(rates, coefs, x_rows.shape[0])
    mixed_f = mixed_in.astype(jnp.float32)
    grad_f = gate_grad.astype(jnp.float32)
    conv_out = (causal_apply(long_filter, mixed_f) + skip * mixed_f).astype(jnp.bfloat16)
    conv_grad = (causal_apply(long_filter, grad_f[::-1])[::-1] + skip * grad_f).astype(jnp.bfloat16)
    conv_f = conv_out.astype(jnp.float32)
    back_f = conv_grad.astype(jnp.float32)
    layer_out = (x_rows + query_rows * conv_f).astype(jnp.bfloat16)
    branch_grads = [grad_out * conv_f, back_f * value_rows, back_f * key_rows]
    normed_grad = jnp.zeros_like(normed)
    for branch in range(3):
        for lag in range(TAPS):
            normed_grad = normed_grad + taps[branch, lag] * advanced(branch_grads[branch], lag)
    scaled = gain * normed_grad
    input_grad = grad_out + inverse * scaled - x_rows * inverse * inverse * inverse * lax.optimization_barrier(jnp.mean(scaled * x_rows, axis=-1, keepdims=True))
    return (layer_out, input_grad.astype(jnp.bfloat16))

def reference(section_input, cotangent, norm_gain, short_filter, decay_rate, residue, skip_gain):
    layer_out, input_grad = lax.map(one_section, (section_input, cotangent, norm_gain, short_filter, decay_rate, residue, skip_gain))
    passed_on = jnp.concatenate([jnp.zeros_like(layer_out[:1]), layer_out[:-1]], axis=0)
    passed_back = jnp.concatenate([input_grad[1:], jnp.zeros_like(input_grad[:1])], axis=0)
    return (passed_on, passed_back)
```

```python
import functools

import jax
import jax.numpy as jnp
import ml_dtypes
import numpy as np
from jax import lax
from jax.experimental import pallas as pl
from jax.experimental.pallas import tpu as pltpu
from jax.sharding import PartitionSpec as P

MODES = 16
NODES = 14
PADDED = 16
LANES = 128
WIDE = 256
F32 = jnp.float32
BF16 = jnp.bfloat16


def node_places(rows):
    k = np.arange(NODES)
    return 0.5 * (rows - 1) * (1.0 - np.cos((2 * k + 1) * np.pi / (2 * NODES)))


def cardinals(rows):
    nodes = node_places(rows)
    lags = np.arange(rows, dtype=np.float64)
    table = np.ones((rows, NODES))
    for k in range(NODES):
        for m in range(NODES):
            if m != k:
                table[:, k] *= (lags - nodes[m]) / (nodes[k] - nodes[m])
    return table


def halves(table):
    high = table.astype(ml_dtypes.bfloat16)
    low = (table - high.astype(np.float64)).astype(ml_dtypes.bfloat16)
    return high, low


def constants(rows):
    table = cardinals(rows)
    padded = np.zeros((rows, PADDED))
    padded[:, :NODES] = table
    high, low = halves(padded)
    flip_high, flip_low = high[::-1], low[::-1]
    moment_ahead = np.concatenate([flip_high.T, flip_low.T], axis=0)
    moment_back = np.concatenate([high.T, low.T], axis=0)
    spread_ahead = np.concatenate([high, low, high], axis=1)
    spread_back = np.concatenate([flip_high, flip_low, flip_high], axis=1)
    lag = np.arange(rows)[:, None] - np.arange(rows)[None, :]
    toeplitz = np.where(lag[:, :, None] >= 0, table[np.maximum(lag, 0)], 0.0)
    near_ahead = np.transpose(toeplitz, (0, 2, 1)).reshape(rows, NODES * rows)
    near_back = np.transpose(toeplitz, (1, 2, 0)).reshape(rows, NODES * rows)
    places = np.zeros((PADDED, LANES), np.float32)
    places[:NODES] = node_places(rows)[:, None]
    cast = ml_dtypes.bfloat16
    return dict(
        moments=np.concatenate([moment_ahead, moment_back], axis=0),
        spread=np.concatenate([spread_ahead, spread_back], axis=0),
        near=np.stack([near_ahead, near_back]).astype(cast),
        places=places,
    )


def tables_kernel(nodes, rates_ref, residue_ref, places_ref, powers_ref, columns_ref, nodal_ref, coef_ref):
    rates = rates_ref[...]
    coef = residue_ref[...] * jnp.sqrt(1.0 - jnp.exp(-2.0 * rates))
    coef_ref[...] = coef
    for k in range(NODES):
        powers_ref[k] = jnp.exp(rates * (-nodes[k]))
    places = jnp.concatenate([places_ref[...]] * (rates.shape[1] // LANES), axis=1)
    nodal = jnp.zeros_like(rates)
    for r in range(MODES):
        column = jnp.exp(-rates[r : r + 1] * places)
        columns_ref[r] = column
        nodal = nodal + column * coef[r : r + 1]
    nodal_ref[...] = nodal


def taps_of(taps_ref, cols):
    return [[taps_ref[3 * j + i : 3 * j + i + 1, cols] for i in range(3)] for j in range(3)]


def filtered(taps, now, past, older):
    return [t[0] * now + t[1] * past + t[2] * older for t in taps]


def start_kernel(
    x_ref, cot_ref, rim_ref, gain_ref, taps_ref, powers_ref, moments_ref,
    mixed_ref, gate_ref, state_ref, inverse_ref, front_ref, normed_ref,
):
    rows, width = x_ref.shape

    def square(i, total):
        x = x_ref[:, pl.ds(pl.multiple_of(i * LANES, LANES), LANES)].astype(F32)
        return total + x * x

    total = lax.fori_loop(0, width // LANES, square, jnp.zeros((rows, LANES), F32))
    inverse = lax.rsqrt(jnp.sum(total, axis=1, keepdims=True) * (1.0 / width) + 1e-06)
    rim_all = rim_ref[...].astype(F32)
    rim_inverse = lax.rsqrt(jnp.sum(rim_all * rim_all, axis=1, keepdims=True) * (1.0 / width) + 1e-06)
    inverse_ref[0:rows] = jnp.broadcast_to(inverse, (rows, LANES))
    inverse_ref[rows : rows + 2] = jnp.broadcast_to(rim_inverse, (2, LANES))
    front_ref[0:2] = x_ref[0:16].astype(F32)[0:2]
    front_ref[2:4] = cot_ref[0:16].astype(F32)[0:2]

    def chunk(i, carry):
        cols = pl.ds(pl.multiple_of(i * WIDE, WIDE), WIDE)
        gain = gain_ref[:, cols]
        now = x_ref[:, cols].astype(F32) * inverse * gain
        normed_ref[8 : rows + 8] = now
        normed_ref[6:8] = rim_ref[:, cols].astype(F32) * rim_inverse * gain
        past = normed_ref[7 : rows + 7]
        older = normed_ref[6 : rows + 6]
        query, key, value = filtered(taps_of(taps_ref, cols), now, past, older)
        mixed = (key * value).astype(BF16)
        gate = (cot_ref[:, cols].astype(F32) * query).astype(BF16)
        mixed_ref[:, cols] = mixed
        gate_ref[:, cols] = gate
        for side, signal in enumerate((mixed, gate)):
            both = jnp.dot(
                moments_ref[32 * side : 32 * side + 32], signal, preferred_element_type=F32
            )
            moment = both[:PADDED] + both[PADDED:]
            state = powers_ref[0, :, cols] * moment[0:1]
            for k in range(1, NODES):
                state = state + powers_ref[k, :, cols] * moment[k : k + 1]
            for h in range(WIDE // LANES):
                state_ref[i * (WIDE // LANES) + h, MODES * side : MODES * (side + 1)] = state[
                    :, h * LANES : (h + 1) * LANES
                ].astype(BF16)
        return carry

    lax.fori_loop(0, width // WIDE, chunk, 0)


def near_kernel(mixed_ref, gate_ref, nodal_ref, skip_ref, near_ref, ahead_ref, back_ref, parts_ref):
    rows = mixed_ref.shape[0]
    nodal = nodal_ref[...].astype(BF16)
    for side, (signal_ref, out_ref) in enumerate(((mixed_ref, ahead_ref), (gate_ref, back_ref))):
        signal = signal_ref[...]
        for k in range(NODES):
            parts_ref[k * rows : (k + 1) * rows] = signal * nodal[k : k + 1]
        out_ref[...] = (
            jnp.dot(near_ref[side], parts_ref[...], preferred_element_type=F32)
            + skip_ref[...] * signal.astype(F32)
        )


def scan_kernel(rates_ref, state_ref, enter_ref, *, rows):
    count = state_ref.shape[0]
    first = lax.axis_index("seq") * LANES
    rates = rates_ref[:, pl.ds(pl.multiple_of(first, LANES), LANES)]
    decay = jnp.exp(rates * (-float(rows)))
    ahead = jnp.zeros((MODES, LANES), F32)
    back = jnp.zeros((MODES, LANES), F32)
    for d in range(count):
        enter_ref[d, 0:MODES] = ahead.astype(BF16)
        ahead = decay * ahead + state_ref[d, 0:MODES].astype(F32)
        e = count - 1 - d
        enter_ref[e, MODES : 2 * MODES] = back.astype(BF16)
        back = decay * back + state_ref[e, MODES : 2 * MODES].astype(F32)


def finish_kernel(
    x_ref, cot_ref, ahead_ref, back_ref, columns_ref, enter_ref, state_ref, coef_ref, rates_ref,
    gain_ref, taps_ref, skip_ref, rim_ref, front_ref, inverse_ref, spread_ref,
    layer_ref, grad_ref,
    normed_ref, one_ref, two_ref, base_ref, total_ref, scale_ref,
):
    step = pl.program_id(0)
    rows, width = x_ref.shape
    inverse = inverse_ref[0:rows, 0:1]

    @pl.when(step == 0)
    def _():
        total_ref[...] = jnp.zeros_like(total_ref)
        after = front_ref[0:2]
        scale = lax.rsqrt(jnp.sum(after * after, axis=1, keepdims=True) * (1.0 / width) + 1e-06)
        scale_ref[0:2] = jnp.broadcast_to(scale, (2, LANES))

    cols = pl.ds(pl.multiple_of(step * WIDE, WIDE), WIDE)
    gain = gain_ref[...]
    skip = skip_ref[...]
    taps = taps_of(taps_ref, slice(None))
    x = x_ref[:, cols].astype(F32)
    cot = cot_ref[...].astype(F32)
    now = x * inverse * gain
    normed_ref[8 : rows + 8] = now
    normed_ref[6:8] = rim_ref[:, cols].astype(F32) * inverse_ref[rows : rows + 2, 0:1] * gain
    normed_ref[rows + 8 : rows + 10] = front_ref[0:2, cols] * scale_ref[0:2, 0:1] * gain
    past = normed_ref[7 : rows + 7]
    older = normed_ref[6 : rows + 6]
    query, key, value = filtered(taps, now, past, older)
    n_query, n_key, n_value = filtered(
        taps, normed_ref[rows + 8 : rows + 10], normed_ref[rows + 7 : rows + 9], normed_ref[rows + 6 : rows + 8]
    )

    coef = coef_ref[...]
    rates = rates_ref[...]
    decay = jnp.exp(-rates)
    lead = coef * decay
    entered = [jnp.concatenate([enter_ref[h, 16 * s : 16 * s + 16].astype(F32) for h in range(WIDE // LANES)], axis=1) for s in range(2)]
    own = jnp.concatenate([state_ref[h, 0:16].astype(F32) for h in range(WIDE // LANES)], axis=1)

    convs = []
    for side, near_ref in enumerate((ahead_ref, back_ref)):
        weight = lead * entered[side]
        nodal = columns_ref[0] * weight[0:1]
        for r in range(1, MODES):
            nodal = nodal + columns_ref[r] * weight[r : r + 1]
        high = nodal.astype(BF16)
        low = (nodal - high.astype(F32)).astype(BF16)
        far = jnp.dot(
            spread_ref[side * rows : (side + 1) * rows],
            jnp.concatenate([high, high, low], axis=0),
            preferred_element_type=F32,
        )
        convs.append((near_ref[...] + far).astype(BF16).astype(F32))
    conv, conv_back = convs

    layer_ref[...] = (x + query * conv).astype(BF16)

    n_cot = front_ref[2:4, cols]
    n_mixed = (n_key * n_value).astype(BF16).astype(F32)
    n_gate = (n_cot * n_query).astype(BF16).astype(F32)
    leave = jnp.exp(rates * (-float(rows))) * entered[0] + own
    over = lambda a: jnp.sum(a, axis=0, keepdims=True)
    direct = over(coef) + skip
    mixed_0, mixed_1 = n_mixed[0:1], n_mixed[1:2]
    gate_0, gate_1 = n_gate[0:1], n_gate[1:2]
    conv_0 = over(lead * leave) + direct * mixed_0
    conv_1 = over(lead * decay * leave) + over(lead) * mixed_0 + direct * mixed_1
    back_0 = over(coef * entered[1]) + skip * gate_0
    back_1 = over(coef * (1.0 / decay) * (entered[1] - gate_0)) + skip * gate_1
    n_conv = jnp.concatenate([conv_0, conv_1], axis=0).astype(BF16).astype(F32)
    n_back = jnp.concatenate([back_0, back_1], axis=0).astype(BF16).astype(F32)

    grads = (cot * conv, conv_back * value, conv_back * key)
    n_grads = (n_cot * n_conv, n_back * n_value, n_back * n_key)
    lagged = [sum(taps[j][i] * grads[j] for j in range(3)) for i in range(3)]
    one_ref[0:rows] = lagged[1]
    two_ref[0:rows] = lagged[2]
    one_ref[rows : rows + 2] = sum(taps[j][1] * n_grads[j] for j in range(3))
    two_ref[rows : rows + 2] = sum(taps[j][2] * n_grads[j] for j in range(3))
    scaled = gain * (lagged[0] + one_ref[1 : rows + 1] + two_ref[2 : rows + 2])
    base_ref[:, cols] = cot + inverse * scaled
    product = scaled * x
    partial = total_ref[...]
    for h in range(WIDE // LANES):
        partial = partial + product[:, h * LANES : (h + 1) * LANES]
    total_ref[...] = partial

    @pl.when(step == pl.num_programs(0) - 1)
    def _():
        mean = jnp.sum(total_ref[...], axis=1, keepdims=True) * (1.0 / width)
        factor = inverse * inverse * inverse * mean

        def emit(i, carry):
            part = pl.ds(pl.multiple_of(i * WIDE, WIDE), WIDE)
            grad_ref[:, part] = (base_ref[:, part] - x_ref[:, part].astype(F32) * factor).astype(BF16)
            return carry

        lax.fori_loop(0, width // WIDE, emit, 0)


def shifted(block, axis, distance):
    devices = range(lax.axis_size(axis))
    route = [(i - distance, i) for i in devices if i - distance in devices]
    return lax.ppermute(block, axis, route)


def whole(shape):
    return pl.BlockSpec(shape, lambda *i: (0,) * len(shape))


def across(shape, step, axis=None):
    axis = len(shape) - 1 if axis is None else axis
    block = shape[:axis] + (step,) + shape[axis + 1 :]
    return pl.BlockSpec(block, lambda i: (0,) * axis + (i,) + (0,) * (len(shape) - axis - 1))


def params(mib):
    return pltpu.CompilerParams(vmem_limit_bytes=mib * 1024 * 1024)


def local(section_input, cotangent, norm_gain, short_filter, decay_rate, residue, skip_gain):
    x = section_input[0]
    cot = cotangent[0]
    rows, width = x.shape
    gain = norm_gain
    taps = short_filter[0].reshape(9, width)
    rates = decay_rate[0]
    weights = residue[0]
    skip = skip_gain
    count = lax.axis_size("seq")
    fixed = constants(rows)
    shape = jax.ShapeDtypeStruct

    rim = shifted(x[rows - 2 :], "seq", 1)

    step = 512
    powers, columns, nodal, coef = pl.pallas_call(
        functools.partial(tables_kernel, [float(p) for p in node_places(rows)]),
        grid=(width // step,),
        in_specs=[across((MODES, width), step), across((MODES, width), step), whole((PADDED, LANES))],
        out_specs=[
            across((NODES, MODES, width), step),
            across((MODES, PADDED, width), step),
            across((PADDED, width), step),
            across((MODES, width), step),
        ],
        out_shape=[
            shape((NODES, MODES, width), F32),
            shape((MODES, PADDED, width), F32),
            shape((PADDED, width), F32),
            shape((MODES, width), F32),
        ],
        compiler_params=params(24),
        name="tables",
    )(rates, weights, jnp.asarray(fixed["places"]))

    mixed, gate, state, inverse, front = pl.pallas_call(
        start_kernel,
        out_shape=[
            shape((rows, width), BF16),
            shape((rows, width), BF16),
            shape((width // LANES, 2 * MODES, LANES), BF16),
            shape((rows + 8, LANES), F32),
            shape((4, width), F32),
        ],
        scratch_shapes=[pltpu.VMEM((rows + 8, WIDE), F32)],
        compiler_params=params(32),
        name="start",
    )(x, cot, rim, gain, taps, powers, jnp.asarray(fixed["moments"]))

    gathered = lax.all_to_all(state, "seq", split_axis=0, concat_axis=0, tiled=True)
    front = shifted(front, "seq", -1)

    ahead, back = pl.pallas_call(
        near_kernel,
        grid=(width // WIDE,),
        in_specs=[
            across((rows, width), WIDE),
            across((rows, width), WIDE),
            across((PADDED, width), WIDE),
            across((1, width), WIDE),
            whole((2, rows, NODES * rows)),
        ],
        out_specs=[across((rows, width), WIDE), across((rows, width), WIDE)],
        out_shape=[shape((rows, width), F32), shape((rows, width), F32)],
        scratch_shapes=[pltpu.VMEM((NODES * rows, WIDE), BF16)],
        compiler_params=params(24),
        cost_estimate=pl.CostEstimate(
            flops=4 * NODES * rows * rows * width, bytes_accessed=7 << 20, transcendentals=0
        ),
        name="near",
    )(mixed, gate, nodal, skip, jnp.asarray(fixed["near"]))

    entering = pl.pallas_call(
        functools.partial(scan_kernel, rows=rows),
        out_shape=shape((count, 2 * MODES, LANES), BF16),
        compiler_params=params(16),
        name="scan",
    )(rates, gathered)
    enter = lax.all_to_all(entering, "seq", split_axis=0, concat_axis=0, tiled=True)

    pieces = WIDE // LANES
    layer_out, input_grad = pl.pallas_call(
        finish_kernel,
        grid=(width // WIDE,),
        in_specs=[
            whole((rows, width)),
            across((rows, width), WIDE),
            across((rows, width), WIDE),
            across((rows, width), WIDE),
            across((MODES, PADDED, width), WIDE),
            across((width // LANES, 2 * MODES, LANES), pieces, 0),
            across((width // LANES, 2 * MODES, LANES), pieces, 0),
            across((MODES, width), WIDE),
            across((MODES, width), WIDE),
            across((1, width), WIDE),
            across((9, width), WIDE),
            across((1, width), WIDE),
            whole((2, width)),
            whole((4, width)),
            whole((rows + 8, LANES)),
            whole((2 * rows, 3 * PADDED)),
        ],
        out_specs=[across((rows, width), WIDE), whole((rows, width))],
        out_shape=[shape((rows, width), BF16), shape((rows, width), BF16)],
        scratch_shapes=[
            pltpu.VMEM((rows + 16, WIDE), F32),
            pltpu.VMEM((rows + 8, WIDE), F32),
            pltpu.VMEM((rows + 8, WIDE), F32),
            pltpu.VMEM((rows, width), F32),
            pltpu.VMEM((rows, LANES), F32),
            pltpu.VMEM((8, LANES), F32),
        ],
        compiler_params=params(32),
        name="finish",
    )(
        x, cot, ahead, back, columns, enter, state, coef, rates,
        gain, taps, skip, rim, front, inverse, jnp.asarray(fixed["spread"]),
    )

    passed_on = shifted(layer_out, "section", 1)
    passed_back = shifted(input_grad, "section", -1)
    return passed_on[None], passed_back[None]


def solution(mesh):
    in_specs = (
        P("section", "seq", None),
        P("section", "seq", None),
        P("section", None),
        P("section", None, None, None),
        P("section", None, None),
        P("section", None, None),
        P("section", None),
    )
    out_specs = (P("section", "seq", None), P("section", "seq", None))
    return jax.shard_map(local, mesh=mesh, in_specs=in_specs, out_specs=out_specs, check_vma=False)
```

```python
import functools

import jax
import jax.numpy as jnp
import ml_dtypes
import numpy as np
from jax import lax
from jax.experimental import pallas as pl
from jax.experimental.pallas import tpu as pltpu
from jax.sharding import PartitionSpec as P

MODES = 16
NODES = 14
PADDED = 16
LANES = 128
START_GROUP = 512
PIECES = 4
NEAR_STEP = 1024
NEAR_GROUP = 512
FINISH_GROUP = 256
F32 = jnp.float32
BF16 = jnp.bfloat16
shape = jax.ShapeDtypeStruct


def node_places(rows):
    k = np.arange(NODES)
    return 0.5 * (rows - 1) * (1.0 - np.cos((2 * k + 1) * np.pi / (2 * NODES)))


def cardinals(rows):
    nodes = node_places(rows)
    lags = np.arange(rows, dtype=np.float64)
    table = np.ones((rows, NODES))
    for k in range(NODES):
        for m in range(NODES):
            if m != k:
                table[:, k] *= (lags - nodes[m]) / (nodes[k] - nodes[m])
    return table


def halves(table):
    high = table.astype(ml_dtypes.bfloat16)
    low = (table - high.astype(np.float64)).astype(ml_dtypes.bfloat16)
    return high, low


def constants(rows):
    table = cardinals(rows)
    padded = np.zeros((rows, PADDED))
    padded[:, :NODES] = table
    high, low = halves(padded)
    flip_high, flip_low = high[::-1], low[::-1]
    moment_ahead = np.concatenate([flip_high.T, flip_low.T], axis=0)
    moment_back = np.concatenate([high.T, low.T], axis=0)
    spread_ahead = np.concatenate([high, low, high], axis=1)
    spread_back = np.concatenate([flip_high, flip_low, flip_high], axis=1)
    lag = np.arange(rows)[:, None] - np.arange(rows)[None, :]
    toeplitz = np.where(lag[:, :, None] >= 0, table[np.maximum(lag, 0)], 0.0)
    near_ahead = np.transpose(toeplitz, (0, 2, 1)).reshape(rows, NODES * rows)
    near_back = np.transpose(toeplitz, (1, 2, 0)).reshape(rows, NODES * rows)
    places = np.zeros((PADDED, LANES), np.float32)
    places[:NODES] = node_places(rows)[:, None]
    cast = ml_dtypes.bfloat16
    return dict(
        moments=np.concatenate([moment_ahead, moment_back], axis=0),
        spread=np.concatenate([spread_ahead, spread_back], axis=0),
        near=np.stack([near_ahead, near_back]).astype(cast),
        places=places,
    )


def coefs_of(rates, residue):
    return residue * jnp.sqrt(1.0 - jnp.exp(-2.0 * rates))


def nodal_sum(rates, weight, places):
    places = wide(places, rates.shape[1])
    total = jnp.exp(-rates[0:1] * places) * weight[0:1]
    for r in range(1, MODES):
        total = total + jnp.exp(-rates[r : r + 1] * places) * weight[r : r + 1]
    return total


def taps_of(taps_ref, cols):
    return [[taps_ref[j, i, :, cols] for i in range(3)] for j in range(3)]


def group_of(index, size=LANES):
    return pl.ds(pl.multiple_of(index * size, size), size)


def wide(block, width):
    return jnp.concatenate([block] * (width // LANES), axis=1)


def row_scale(block_sum, width):
    return lax.rsqrt(jnp.sum(block_sum, axis=1, keepdims=True) * (1.0 / width) + 1e-06)


def lane_sums(block):
    total = block[:, :LANES]
    for i in range(1, block.shape[1] // LANES):
        total = total + block[:, i * LANES : (i + 1) * LANES]
    return total


def filtered(taps, now, past, older):
    return [t[0] * now + t[1] * past + t[2] * older for t in taps]


def start_kernel(
    nodes, x_hbm, cot_hbm, gain_hbm, taps_hbm, rates_hbm, moments_ref,
    mixed_hbm, gate_hbm, state_ref, inverse_ref,
    x_ref, cot_ref, gain_ref, taps_ref, rates_ref, mixed_ref, gate_ref, normed_ref, moment_ref,
    x_sems, cot_sems, table_sems, mixed_sems, gate_sems,
):
    rows, width = x_ref.shape
    size = START_GROUP
    pieces = x_sems.shape[0]
    part = width // pieces

    def piece(p):
        return slice(None), pl.ds(p * part, part)

    x_copies = [pltpu.make_async_copy(x_hbm.at[piece(p)], x_ref.at[piece(p)], x_sems.at[p]) for p in range(pieces)]
    cot_copies = [
        pltpu.make_async_copy(cot_hbm.at[piece(p)], cot_ref.at[piece(p)], cot_sems.at[p]) for p in range(pieces)
    ]
    table_copies = [
        pltpu.make_async_copy(source, target, table_sems.at[n])
        for n, (source, target) in enumerate(((gain_hbm, gain_ref), (taps_hbm, taps_ref), (rates_hbm, rates_ref)))
    ]
    for copy in x_copies + table_copies + cot_copies:
        copy.start()

    normed_ref[0:8] = jnp.zeros((8, size), F32)
    total = jnp.zeros((rows, LANES), F32)
    for p in range(pieces):
        x_copies[p].wait()

        def square(i, total):
            x = x_ref[:, group_of(p * (part // size) + i, size)].astype(F32)
            return total + lane_sums(x * x)

        total = lax.fori_loop(0, part // size, square, total)
    inverse_ref[...] = jnp.broadcast_to(row_scale(total, width), (rows, LANES))
    for copy in table_copies:
        copy.wait()

    def group(i, carry):
        cols = group_of(i, size)
        now = x_ref[:, cols].astype(F32) * wide(inverse_ref[...], size) * gain_ref[:, cols]
        normed_ref[8 : rows + 8] = now
        past = normed_ref[7 : rows + 7]
        older = normed_ref[6 : rows + 6]
        query, key, value = filtered(taps_of(taps_ref, cols), now, past, older)
        kept = lax.broadcasted_iota(jnp.int32, (16, size), 0) >= 2
        for side, (signal, out_ref) in enumerate(
            ((key * value, mixed_ref), (cot_ref[:, cols].astype(F32) * query, gate_ref))
        ):
            head = jnp.where(kept, signal[0:16], 0.0)
            signal = jnp.concatenate([head, signal[16:]], axis=0).astype(BF16)
            out_ref[:, cols] = signal
            both = jnp.dot(moments_ref[32 * side : 32 * side + 32], signal, preferred_element_type=F32)
            moment_ref[PADDED * side : PADDED * (side + 1), cols] = both[:PADDED] + both[PADDED:]
        return carry

    def project(i, carry):
        cols = group_of(i)
        rates = rates_ref[:, cols]
        states = [0.0, 0.0]
        for k in range(NODES):
            power = jnp.exp(rates * (-nodes[k]))
            states = [
                states[side] + power * moment_ref[PADDED * side + k : PADDED * side + k + 1, cols]
                for side in range(2)
            ]
        for side in range(2):
            state_ref[MODES * side : MODES * (side + 1), cols] = states[side]
        return carry

    out_copies = []
    for p in range(pieces):
        cot_copies[p].wait()
        lax.fori_loop(p * (part // size), (p + 1) * (part // size), group, 0)
        out_copies += [
            pltpu.make_async_copy(mixed_ref.at[piece(p)], mixed_hbm.at[piece(p)], mixed_sems.at[p]),
            pltpu.make_async_copy(gate_ref.at[piece(p)], gate_hbm.at[piece(p)], gate_sems.at[p]),
        ]
        for copy in out_copies[-2:]:
            copy.start()
    lax.fori_loop(0, width // LANES, project, 0, unroll=2)
    for copy in out_copies:
        copy.wait()


def edge_kernel(
    x_ref, cot_ref, rim_ref, gain_ref, taps_ref, rates_ref, part_ref, inverse_ref,
    head_ref, state_ref, rim_scale_ref, front_ref, normed_ref, *, rows,
):
    width = x_ref.shape[1]
    rim = rim_ref[...].astype(F32)
    scale = row_scale(lane_sums(rim * rim), width)
    rim_scale_ref[0:2] = jnp.broadcast_to(scale, (2, LANES))
    front_ref[0:2] = x_ref[...].astype(F32)[0:2]
    front_ref[2:4] = cot_ref[...].astype(F32)[0:2]
    part = 4 * LANES

    def chunk(i, carry):
        cols = pl.ds(pl.multiple_of(i * part, part), part)
        gain = gain_ref[:, cols]
        now = x_ref[:, cols].astype(F32) * wide(inverse_ref[...], part) * gain
        normed_ref[8:24] = now
        normed_ref[6:8] = rim_ref[:, cols].astype(F32) * scale * gain
        taps = taps_of(taps_ref, cols)
        query, key, value = filtered(taps, now, normed_ref[7:23], normed_ref[6:22])
        mixed = (key * value).astype(BF16)
        gate = (cot_ref[:, cols].astype(F32) * query).astype(BF16)
        head_ref[0, :, cols] = mixed
        head_ref[1, :, cols] = gate
        rates = rates_ref[:, cols]
        mixed = mixed.astype(F32)
        gate = gate.astype(F32)
        ahead = (
            part_ref[0:MODES, cols]
            + jnp.exp(rates * (1.0 - rows)) * mixed[0:1]
            + jnp.exp(rates * (2.0 - rows)) * mixed[1:2]
        )
        back = part_ref[MODES : 2 * MODES, cols] + gate[0:1] + jnp.exp(-rates) * gate[1:2]
        for side, state in enumerate((ahead, back)):
            for h in range(part // LANES):
                state_ref[i * (part // LANES) + h, MODES * side : MODES * (side + 1)] = state[
                    :, h * LANES : (h + 1) * LANES
                ].astype(BF16)
        return carry

    lax.fori_loop(0, width // part, chunk, 0)


def near_kernel(
    signal_ref, head_ref, rates_ref, residue_ref, places_ref, skip_ref, near_ref, mark_ref, out_ref, done_ref, parts_ref
):
    rows = signal_ref.shape[0]
    done_ref[...] = jnp.zeros_like(done_ref)
    size = min(NEAR_GROUP, signal_ref.shape[1])

    def group(i, carry):
        cols = group_of(i, size)
        rates = rates_ref[:, cols]
        nodal = nodal_sum(rates, coefs_of(rates, residue_ref[:, cols]), places_ref[...]).astype(BF16)
        signal = jnp.concatenate([head_ref[0, :, cols], signal_ref[16:, cols]], axis=0)
        for k in range(NODES):
            parts_ref[k * rows : (k + 1) * rows] = signal * nodal[k : k + 1]
        out_ref[:, cols] = (
            jnp.dot(near_ref[0], parts_ref[...], preferred_element_type=F32)
            + skip_ref[:, cols] * signal.astype(F32)
        )
        return carry

    lax.fori_loop(0, signal_ref.shape[1] // size, group, 0)


def scan_kernel(rates_ref, state_ref, mark_ref, enter_ref, done_ref, *, rows):
    done_ref[...] = jnp.zeros_like(done_ref)
    count = state_ref.shape[0]
    first = lax.axis_index("seq") * LANES
    rates = rates_ref[:, pl.ds(pl.multiple_of(first, LANES), LANES)]
    decay = jnp.exp(rates * (-float(rows)))
    ahead = jnp.zeros((MODES, LANES), F32)
    back = jnp.zeros((MODES, LANES), F32)
    for d in range(count):
        enter_ref[d, 0:MODES] = ahead.astype(BF16)
        ahead = decay * ahead + state_ref[d, 0:MODES].astype(F32)
        e = count - 1 - d
        enter_ref[e, MODES : 2 * MODES] = back.astype(BF16)
        back = decay * back + state_ref[e, MODES : 2 * MODES].astype(F32)


def nodal_kernel_part(i, size, rates_ref, residue_ref, places_ref, enter_ref, nodal_ref):
    cols = group_of(i, size)
    pieces = size // LANES
    rates = rates_ref[:, cols]
    lead = coefs_of(rates, residue_ref[:, cols]) * jnp.exp(-rates)
    places = wide(places_ref[...], size)
    weights = []
    for side in range(2):
        entered = [enter_ref[i * pieces + h, MODES * side : MODES * (side + 1)].astype(F32) for h in range(pieces)]
        weights.append(lead * jnp.concatenate(entered, axis=1))
    nodals = [0.0, 0.0]
    for r in range(MODES):
        column = jnp.exp(-rates[r : r + 1] * places)
        nodals = [nodals[side] + column * weights[side][r : r + 1] for side in range(2)]
    for side in range(2):
        high = nodals[side].astype(BF16)
        low = (nodals[side] - high.astype(F32)).astype(BF16)
        nodal_ref[side, :, cols] = jnp.concatenate([high, high, low], axis=0)


def finish_kernel(
    rows, first, last, x_hbm, cot_hbm, ahead_hbm, back_hbm, rim_ref, rim_scale_ref, inverse_ref,
    gain_ref, taps_ref, spread_ref, *refs,
):
    if last:
        (places_ref, enter_ref, state_ref, residue_ref, rates_ref, skip_ref, front_ref) = refs[:7]
        refs = refs[7:]
        layer_hbm, grad_hbm, nodal_ref, after_ref = refs[:4]
        refs = refs[4:]
    else:
        nodal_ref, after_ref, layer_hbm, grad_hbm = refs[:4]
        refs = refs[4:]
    (
        x_ref, cot_ref, ahead_ref, back_ref, layer_ref, grad_ref, base_ref, normed_ref, one_ref, two_ref, total_ref,
        load_sems, layer_sems, grad_sems,
    ) = refs
    width = x_ref.shape[1]
    count = cot_ref.shape[0]
    size = min(FINISH_GROUP, width)
    pieces = layer_sems.shape[0]
    part = width // pieces
    top = 16 if first > 0 else 0

    def lanes(p):
        return pl.ds(p * part, part)

    loads = []
    for p in range(pieces):
        loads.append([
            pltpu.make_async_copy(source.at[pl.ds(lo, n), lanes(p)], target.at[:, lanes(p)], load_sems.at[k, p])
            for k, (source, target, lo, n) in enumerate((
                (x_hbm, x_ref, first - top, count + top),
                (cot_hbm, cot_ref, first, count),
                (ahead_hbm, ahead_ref, first, count),
                (back_hbm, back_ref, first, count),
            ))
        ])
        for copy in loads[p]:
            copy.start()

    total_ref[...] = jnp.zeros_like(total_ref)
    if last:
        def fill(i, carry):
            nodal_kernel_part(i, size, rates_ref, residue_ref, places_ref, enter_ref, nodal_ref)
            return carry

        lax.fori_loop(0, width // size, fill, 0)
        following = front_ref[0:2]
        after_scale = row_scale(lane_sums(following * following), width)

    inverse = wide(inverse_ref[first : first + count], size)

    def group(i, carry):
        cols = group_of(i, size)
        gain = gain_ref[:, cols]
        taps = taps_of(taps_ref, cols)
        x = x_ref[top:, cols].astype(F32)
        cot = cot_ref[:, cols].astype(F32)
        normed_ref[16 : count + 16] = x * inverse * gain
        if first > 0:
            above = x_ref[0:16, cols].astype(F32)
            normed_ref[0:16] = above * wide(inverse_ref[first - 16 : first], size) * gain
        else:
            normed_ref[14:16] = rim_ref[:, cols].astype(F32) * wide(rim_scale_ref[0:2], size) * gain
        now = normed_ref[16 : count + 16]
        past = normed_ref[15 : count + 15]
        older = normed_ref[14 : count + 14]
        query, key, value = filtered(taps, now, past, older)

        convs = []
        for side, near_ref in enumerate((ahead_ref, back_ref)):
            far = jnp.dot(
                spread_ref[side * rows + first : side * rows + first + count],
                nodal_ref[side, :, cols],
                preferred_element_type=F32,
            )
            convs.append((near_ref[:, cols] + far).astype(BF16).astype(F32))
        conv, conv_back = convs
        layer_ref[:, cols] = (x + query * conv).astype(BF16)

        grads = (cot * conv, conv_back * value, conv_back * key)
        lagged = [sum(taps[j][i] * grads[j] for j in range(3)) for i in range(3)]
        one_ref[0:count] = lagged[1]
        two_ref[0:count] = lagged[2]
        if last:
            normed_ref[count + 16 : count + 18] = front_ref[0:2, cols] * after_scale * gain
            n_query, n_key, n_value = filtered(
                taps,
                normed_ref[count + 16 : count + 18],
                normed_ref[count + 15 : count + 17],
                normed_ref[count + 14 : count + 16],
            )
            n_cot = front_ref[2:4, cols]
            n_mixed = (n_key * n_value).astype(BF16).astype(F32)
            n_gate = (n_cot * n_query).astype(BF16).astype(F32)
            rates = rates_ref[:, cols]
            coef = coefs_of(rates, residue_ref[:, cols])
            decay = jnp.exp(-rates)
            lead = coef * decay
            skip = skip_ref[:, cols]
            blocks = range(size // LANES)
            start = i * (size // LANES)
            entered = [
                jnp.concatenate(
                    [enter_ref[start + h, MODES * s : MODES * (s + 1)].astype(F32) for h in blocks], axis=1
                )
                for s in range(2)
            ]
            own = jnp.concatenate([state_ref[start + h, 0:MODES].astype(F32) for h in blocks], axis=1)
            leave = jnp.exp(rates * (-float(rows))) * entered[0] + own
            over = lambda a: jnp.sum(a, axis=0, keepdims=True)
            direct = over(coef) + skip
            mixed_0, mixed_1 = n_mixed[0:1], n_mixed[1:2]
            gate_0, gate_1 = n_gate[0:1], n_gate[1:2]
            conv_0 = over(lead * leave) + direct * mixed_0
            conv_1 = over(lead * decay * leave) + over(lead) * mixed_0 + direct * mixed_1
            back_0 = over(coef * entered[1]) + skip * gate_0
            back_1 = over(coef * (1.0 / decay) * (entered[1] - gate_0)) + skip * gate_1
            n_conv = jnp.concatenate([conv_0, conv_1], axis=0).astype(BF16).astype(F32)
            n_back = jnp.concatenate([back_0, back_1], axis=0).astype(BF16).astype(F32)
            n_grads = (n_cot * n_conv, n_back * n_value, n_back * n_key)
            one_ref[count : count + 2] = sum(taps[j][1] * n_grads[j] for j in range(3))
            two_ref[count : count + 2] = sum(taps[j][2] * n_grads[j] for j in range(3))
            after_ref[0:8, cols] = lagged[1][0:8]
            after_ref[8:16, cols] = lagged[2][0:8]
        else:
            one_ref[count : count + 8] = after_ref[0:8, cols]
            two_ref[count : count + 8] = after_ref[8:16, cols]
        scaled = gain * (lagged[0] + one_ref[1 : count + 1] + two_ref[2 : count + 2])
        base_ref[:, cols] = cot + inverse * scaled
        total_ref[...] = total_ref[...] + lane_sums(scaled * x)
        return carry

    outs = []
    for p in range(pieces):
        for copy in loads[p]:
            copy.wait()
        lax.fori_loop(p * (part // size), (p + 1) * (part // size), group, 0)
        outs.append(pltpu.make_async_copy(layer_ref.at[:, lanes(p)], layer_hbm.at[:, lanes(p)], layer_sems.at[p]))
        outs[-1].start()

    mean = jnp.sum(total_ref[...], axis=1, keepdims=True) * (1.0 / width)
    scale = inverse_ref[first : first + count]
    factor = wide(scale * scale * scale * jnp.broadcast_to(mean, (count, LANES)), size)

    def emit(i, carry):
        cols = group_of(i, size)
        grad_ref[:, cols] = (base_ref[:, cols] - x_ref[top:, cols].astype(F32) * factor).astype(BF16)
        return carry

    for p in range(pieces):
        lax.fori_loop(p * (part // size), (p + 1) * (part // size), emit, 0)
        outs.append(pltpu.make_async_copy(grad_ref.at[:, lanes(p)], grad_hbm.at[:, lanes(p)], grad_sems.at[p]))
        outs[-1].start()
    for copy in outs:
        copy.wait()


def join_kernel(first, layer_ref, grad_ref, *refs):
    layer_hbm, grad_hbm, sems = refs[-3:]
    count = layer_ref.shape[0]
    half = layer_ref.shape[1] // 2
    copies = []
    for n, (source, target) in enumerate(((layer_ref, layer_hbm), (grad_ref, grad_hbm))):
        for h in range(2):
            lanes = pl.ds(h * half, half)
            copies.append(
                pltpu.make_async_copy(source.at[:, lanes], target.at[pl.ds(first, count), lanes], sems.at[n, h])
            )
    for copy in copies:
        copy.start()
    for copy in copies:
        copy.wait()


def shifted(block, axis, distance):
    devices = range(lax.axis_size(axis))
    route = [(i - distance, i) for i in devices if i - distance in devices]
    return lax.ppermute(block, axis, route)


def whole(shape):
    return pl.BlockSpec(shape, lambda *i: (0,) * len(shape))


def across(shape, step, axis=None):
    axis = len(shape) - 1 if axis is None else axis
    block = shape[:axis] + (step,) + shape[axis + 1 :]
    return pl.BlockSpec(block, lambda i: (0,) * axis + (i,) + (0,) * (len(shape) - axis - 1))


def params(mib):
    return pltpu.CompilerParams(vmem_limit_bytes=mib << 20)


def stay(array):
    return pltpu.with_memory_space_constraint(array, pltpu.HBM)


def takes(micros):
    return pl.CostEstimate(
        flops=int(micros * 1.1e9), bytes_accessed=int(micros * 3.5e6), transcendentals=0
    )


def start_call(x, cot, gain, taps, rates, moments):
    rows, width = x.shape
    pieces = PIECES
    far = pl.BlockSpec(memory_space=pltpu.HBM)
    near = pl.BlockSpec(memory_space=pltpu.VMEM)
    return pl.pallas_call(
        functools.partial(start_kernel, [float(p) for p in node_places(rows)]),
        in_specs=[far, far, far, far, far, near],
        out_specs=[far, far, near, near],
        out_shape=[
            shape(x.shape, BF16), shape(x.shape, BF16), shape((2 * MODES, width), F32), shape((rows, LANES), F32),
        ],
        scratch_shapes=[
            pltpu.VMEM(x.shape, BF16),
            pltpu.VMEM(x.shape, BF16),
            pltpu.VMEM(gain.shape, F32),
            pltpu.VMEM(taps.shape, F32),
            pltpu.VMEM(rates.shape, F32),
            pltpu.VMEM(x.shape, BF16),
            pltpu.VMEM(x.shape, BF16),
            pltpu.VMEM((rows + 8, START_GROUP), F32),
            pltpu.VMEM((2 * PADDED, width), F32),
            pltpu.SemaphoreType.DMA((pieces,)),
            pltpu.SemaphoreType.DMA((pieces,)),
            pltpu.SemaphoreType.DMA((3,)),
            pltpu.SemaphoreType.DMA((pieces,)),
            pltpu.SemaphoreType.DMA((pieces,)),
        ],
        compiler_params=params(16),
        cost_estimate=takes(6),
        name="start",
    )(stay(x), stay(cot), stay(gain), stay(taps), stay(rates), moments)


def edge_call(x, cot, rim, gain, taps, rates, part, inverse):
    rows, width = x.shape
    return pl.pallas_call(
        functools.partial(edge_kernel, rows=rows),
        grid=(1,),
        in_specs=[
            whole((16, width)), whole((16, width)), whole(rim.shape), whole(gain.shape), whole(taps.shape),
            whole(rates.shape), whole(part.shape), whole((16, LANES)),
        ],
        out_specs=[
            whole((2, 16, width)), whole((width // LANES, 2 * MODES, LANES)), whole((8, LANES)), whole((4, width)),
        ],
        out_shape=[
            shape((2, 16, width), BF16),
            shape((width // LANES, 2 * MODES, LANES), BF16),
            shape((8, LANES), F32),
            shape((4, width), F32),
        ],
        scratch_shapes=[pltpu.VMEM((24, 4 * LANES), F32)],
        compiler_params=params(6),
        cost_estimate=takes(2),
        name="edge",
    )(x, cot, rim, gain, taps, rates, part, inverse)


def near_call(side, signal, head, rates, residue, places, skip, near, mark):
    rows, width = signal.shape
    step = min(NEAR_STEP, width)
    return pl.pallas_call(
        near_kernel,
        grid=(width // step,),
        in_specs=[
            across(signal.shape, step),
            pl.BlockSpec((1, 16, step), lambda i: (side, 0, i)),
            across(rates.shape, step), across(rates.shape, step), whole(places.shape),
            across(skip.shape, step),
            pl.BlockSpec((1,) + near.shape[1:], lambda i: (side, 0, 0)),
            whole(mark.shape),
        ],
        out_specs=[across(signal.shape, step), whole((8, LANES))],
        out_shape=[pltpu.HBM(signal.shape, F32), shape((8, LANES), F32)],
        scratch_shapes=[pltpu.VMEM((NODES * rows, min(NEAR_GROUP, width)), BF16)],
        compiler_params=params(16),
        cost_estimate=takes(4),
        name="near",
    )(stay(signal), head, rates, residue, places, skip, stay(near), mark)


def scan_call(rates, gathered, mark, rows):
    return pl.pallas_call(
        functools.partial(scan_kernel, rows=rows),
        out_shape=[shape(gathered.shape, BF16), shape((8, LANES), F32)],
        compiler_params=params(6),
        cost_estimate=takes(1),
        name="scan",
    )(rates, gathered, mark)


def finish_call(rows, first, last, tables, *arrays):
    x = arrays[0]
    width = x.shape[1]
    count = rows // 2
    pieces = PIECES
    size = min(FINISH_GROUP, width)
    top = 16 if first > 0 else 0
    far = pl.BlockSpec(memory_space=pltpu.HBM)
    near = pl.BlockSpec(memory_space=pltpu.VMEM)
    half = shape((count, width), BF16)
    out_specs = [far, far]
    out_shape = [half, half]
    if last:
        out_specs += [near, near]
        out_shape += [shape((2, 3 * PADDED, width), BF16), shape((16, width), F32)]
    return pl.pallas_call(
        functools.partial(finish_kernel, rows, first, last),
        in_specs=[far] * 4 + [near] * (len(arrays) - 4 + len(tables)),
        out_specs=out_specs,
        out_shape=out_shape,
        scratch_shapes=[
            pltpu.VMEM((count + top, width), BF16),
            pltpu.VMEM((count, width), BF16),
            pltpu.VMEM((count, width), F32),
            pltpu.VMEM((count, width), F32),
            pltpu.VMEM((count, width), BF16),
            pltpu.VMEM((count, width), BF16),
            pltpu.VMEM((count, width), F32),
            pltpu.VMEM((count + 24, size), F32),
            pltpu.VMEM((count + 8, size), F32),
            pltpu.VMEM((count + 8, size), F32),
            pltpu.VMEM((count, LANES), F32),
            pltpu.SemaphoreType.DMA((4, pieces)),
            pltpu.SemaphoreType.DMA((pieces,)),
            pltpu.SemaphoreType.DMA((pieces,)),
        ],
        compiler_params=params(24),
        cost_estimate=takes(6),
        name="finish",
    )(*[stay(array) for array in arrays[:4]], *arrays[4:], *tables)


def join_call(rows, first, layer, grad, *wholes):
    far = pl.BlockSpec(memory_space=pltpu.HBM)
    near = pl.BlockSpec(memory_space=pltpu.VMEM)
    out = shape((rows, layer.shape[1]), BF16)
    return pl.pallas_call(
        functools.partial(join_kernel, first),
        in_specs=[near, near] + [far] * len(wholes),
        out_specs=[far, far],
        out_shape=[out, out],
        scratch_shapes=[pltpu.SemaphoreType.DMA((2, 2))],
        input_output_aliases={2 + n: n for n in range(len(wholes))},
        compiler_params=params(4),
        cost_estimate=takes(1),
        name="join",
    )(layer, grad, *wholes)


def local(section_input, cotangent, norm_gain, short_filter, decay_rate, residue, skip_gain):
    x = section_input[0]
    cot = cotangent[0]
    rows = x.shape[0]
    taps = jnp.transpose(short_filter, (1, 2, 0, 3))
    rates = decay_rate[0]
    fixed = {name: jnp.asarray(table) for name, table in constants(rows).items()}

    rim = shifted(x[rows - 2 :], "seq", 1)
    weights = residue[0]
    mixed, gate, part, inverse = start_call(x, cot, norm_gain, taps, rates, fixed["moments"])
    head, state, rim_scale, front = edge_call(x, cot, rim, norm_gain, taps, rates, part, inverse)

    gathered = lax.all_to_all(state, "seq", split_axis=0, concat_axis=0, tiled=True)
    front = shifted(front, "seq", -1)
    near = (rates, weights, fixed["places"], skip_gain, fixed["near"])
    ahead, mark = near_call(0, mixed, head, *near, inverse[0:8])
    entering, mark = scan_call(rates, gathered, mark, rows)
    enter = lax.all_to_all(entering, "seq", split_axis=0, concat_axis=0, tiled=True)

    back, mark = near_call(1, gate, head, *near, mark)

    common = (x, cot, ahead, back, rim, rim_scale, inverse, norm_gain, taps, fixed["spread"])
    tables = (fixed["places"], enter, state, weights, rates, skip_gain, front)
    layer, grad, nodal, after = finish_call(rows, rows // 2, True, tables, *common)
    on_high = shifted(layer, "section", 1)
    back_high = shifted(grad, "section", -1)
    layer, grad = finish_call(rows, 0, False, (nodal, after), *common)
    on_low = shifted(layer, "section", 1)
    back_low = shifted(grad, "section", -1)
    joined = join_call(rows, rows // 2, on_high, back_high)
    passed_on, passed_back = join_call(rows, 0, on_low, back_low, *joined)
    return passed_on[None], passed_back[None]


def solution(mesh):
    in_specs = (
        P("section", "seq", None),
        P("section", "seq", None),
        P("section", None),
        P("section", None, None, None),
        P("section", None, None),
        P("section", None, None),
        P("section", None),
    )
    out_specs = (P("section", "seq", None), P("section", "seq", None))
    return jax.shard_map(local, mesh=mesh, in_specs=in_specs, out_specs=out_specs, check_vma=False)
```

```python
import functools

import jax
import jax.numpy as jnp
import ml_dtypes
import numpy as np
from jax import lax
from jax.experimental import pallas as pl
from jax.experimental.pallas import tpu as pltpu
from jax.sharding import PartitionSpec as P

MODES = 16
NODES = 14
PADDED = 16
PACKET = 40
EXTRA = 32
LANES = 128
START_GROUP = 1024
PIECES = 4
SPLIT = 80
NEAR_STEP = 1024
NEAR_GROUP = 1024
FINISH_GROUP = 128
FINISH_TOGETHER = 8
FILL_GROUP = 512
F32 = jnp.float32
BF16 = jnp.bfloat16
shape = jax.ShapeDtypeStruct


def node_places(rows):
    k = np.arange(NODES)
    return 0.5 * (rows - 1) * (1.0 - np.cos((2 * k + 1) * np.pi / (2 * NODES)))


def cardinals(rows):
    nodes = node_places(rows)
    lags = np.arange(rows, dtype=np.float64)
    table = np.ones((rows, NODES))
    for k in range(NODES):
        for m in range(NODES):
            if m != k:
                table[:, k] *= (lags - nodes[m]) / (nodes[k] - nodes[m])
    return table


def halves(table):
    high = table.astype(ml_dtypes.bfloat16)
    low = (table - high.astype(np.float64)).astype(ml_dtypes.bfloat16)
    return high, low


def constants(rows):
    table = cardinals(rows)
    padded = np.zeros((rows, PADDED))
    padded[:, :NODES] = table
    high, low = halves(padded)
    flip_high, flip_low = high[::-1], low[::-1]
    moment_ahead = np.concatenate([flip_high.T, flip_low.T], axis=0)
    moment_back = np.concatenate([high.T, low.T], axis=0)
    spread_ahead = np.concatenate([high, low, high], axis=1)
    spread_back = np.concatenate([flip_high, flip_low, flip_high], axis=1)
    lag = np.arange(rows)[:, None] - np.arange(rows)[None, :]
    toeplitz = np.where(lag[:, :, None] >= 0, table[np.maximum(lag, 0)], 0.0)
    near_ahead = np.transpose(toeplitz, (0, 2, 1)).reshape(rows, NODES * rows)
    near_back = np.transpose(toeplitz, (1, 2, 0)).reshape(rows, NODES * rows)
    places = np.zeros((PADDED, LANES), np.float32)
    places[:NODES] = node_places(rows)[:, None]
    cast = ml_dtypes.bfloat16
    return dict(
        moments=np.concatenate(
            [
                np.concatenate([moment_ahead, np.zeros_like(moment_ahead)], axis=1),
                np.concatenate([np.zeros_like(moment_back), moment_back], axis=1),
            ],
            axis=0,
        ),
        spread=np.concatenate([spread_ahead, spread_back], axis=0),
        near=np.stack([near_ahead, near_back]).astype(cast),
        places=places,
    )


def coefs_of(rates, residue):
    return residue * jnp.sqrt(1.0 - jnp.exp(-2.0 * rates))


def nodal_sum(rates, weight, places):
    places = wide(places, rates.shape[1])
    total = jnp.exp(-rates[0:1] * places) * weight[0:1]
    for r in range(1, MODES):
        total = total + jnp.exp(-rates[r : r + 1] * places) * weight[r : r + 1]
    return total


def taps_of(taps_ref, gain_ref, cols):
    gain = gain_ref[:, cols]
    return [[taps_ref[j, i, :, cols] * gain for i in range(3)] for j in range(3)]


def group_of(index, size=LANES):
    return pl.ds(pl.multiple_of(index * size, size), size)


def wide(block, width):
    return jnp.concatenate([block] * (width // LANES), axis=1)


def row_scale(block_sum, width):
    return lax.rsqrt(jnp.sum(block_sum, axis=1, keepdims=True) * (1.0 / width) + 1e-06)


def lane_sums(block):
    total = block[:, :LANES]
    for i in range(1, block.shape[1] // LANES):
        total = total + block[:, i * LANES : (i + 1) * LANES]
    return total


def filtered(taps, now, past, older):
    return [t[0] * now + t[1] * past + t[2] * older for t in taps]


def start_kernel(
    nodes, x_hbm, cot_hbm, gain_hbm, taps_hbm, rates_hbm, moments_hbm,
    mixed_hbm, gate_hbm, packet_hbm, state_hbm, inverse_hbm,
    x_ref, cot_ref, gain_ref, taps_ref, rates_ref, moments_ref, mixed_ref, gate_ref, packet_ref, state_ref, inverse_ref,
    normed_ref, moment_ref, x_sems, cot_sems, table_sems, mixed_sems, gate_sems, last_sems,
):
    rows, width = x_ref.shape
    size = normed_ref.shape[1]
    pieces = x_sems.shape[0]
    part = width // pieces

    def piece(p):
        return slice(None), pl.ds(p * part, part)

    x_copies = [pltpu.make_async_copy(x_hbm.at[piece(p)], x_ref.at[piece(p)], x_sems.at[p]) for p in range(pieces)]
    cot_copies = [
        pltpu.make_async_copy(cot_hbm.at[piece(p)], cot_ref.at[piece(p)], cot_sems.at[p]) for p in range(pieces)
    ]
    table_copies = [
        pltpu.make_async_copy(source, target, table_sems.at[n])
        for n, (source, target) in enumerate(
            ((gain_hbm, gain_ref), (taps_hbm, taps_ref), (moments_hbm, moments_ref), (rates_hbm, rates_ref))
        )
    ]
    for copy in x_copies + table_copies + cot_copies:
        copy.start()

    normed_ref[0:8] = jnp.zeros((8, size), F32)
    total = jnp.zeros((rows, LANES), F32)
    for p in range(pieces):
        x_copies[p].wait()

        def square(i, total):
            x = x_ref[:, group_of(p * (part // size) + i, size)].astype(F32)
            return total + lane_sums(x * x)

        total = lax.fori_loop(0, part // size, square, total)
    inverse_ref[...] = jnp.broadcast_to(row_scale(total, width), (rows, LANES))
    for copy in table_copies:
        copy.wait()

    def group(i, carry):
        cols = group_of(i, size)
        now = x_ref[:, cols].astype(F32) * wide(inverse_ref[...], size)
        normed_ref[8 : rows + 8] = now
        past = normed_ref[7 : rows + 7]
        older = normed_ref[6 : rows + 6]
        query, key, value = filtered(taps_of(taps_ref, gain_ref, cols), now, past, older)
        kept = lax.broadcasted_iota(jnp.int32, (16, size), 0) >= 2
        signals = []
        for signal, out_ref in ((key * value, mixed_ref), (cot_ref[:, cols].astype(F32) * query, gate_ref)):
            head = jnp.where(kept, signal[0:16], 0.0)
            signal = jnp.concatenate([head, signal[16:]], axis=0).astype(BF16)
            out_ref[:, cols] = signal
            signals.append(signal)
        both = jnp.dot(moments_ref[...], jnp.concatenate(signals, axis=0), preferred_element_type=F32)
        for side in range(2):
            high = 2 * PADDED * side
            moment_ref[PADDED * side : PADDED * (side + 1), cols] = (
                both[high : high + PADDED] + both[high + PADDED : high + 2 * PADDED]
            )
        return carry

    def project(i, carry):
        cols = group_of(i)
        rates = rates_ref[:, cols]
        states = [0.0, 0.0]
        for k in range(NODES):
            power = jnp.exp(rates * (-nodes[k]))
            states = [
                states[side] + power * moment_ref[PADDED * side + k : PADDED * side + k + 1, cols]
                for side in range(2)
            ]
        for side in range(2):
            state_ref[MODES * side : MODES * (side + 1), cols] = states[side]
        x_head = x_ref[0:16, cols].astype(F32)
        x_tail = x_ref[rows - 16 : rows, cols].astype(F32)
        cot_head = cot_ref[0:16, cols].astype(F32)
        packet_ref[i] = jnp.concatenate(
            states + [x_head[0:2], x_tail[14:16], cot_head[0:2], scales], axis=0
        ).astype(BF16)
        return carry

    lane = lax.broadcasted_iota(jnp.int32, (1, LANES), 1)
    scale = jnp.zeros((1, LANES), F32)
    for n, row in enumerate((0, 1, rows - 2, rows - 1)):
        scale = jnp.where(lane == n, inverse_ref[row : row + 1], scale)
    scale_high = scale.astype(BF16).astype(F32)
    scales = jnp.concatenate([scale_high, scale - scale_high], axis=0)

    out_copies = []
    for p in range(pieces):
        cot_copies[p].wait()
        lax.fori_loop(p * (part // size), (p + 1) * (part // size), group, 0)
        out_copies += [
            pltpu.make_async_copy(mixed_ref.at[piece(p)], mixed_hbm.at[piece(p)], mixed_sems.at[p]),
            pltpu.make_async_copy(gate_ref.at[piece(p)], gate_hbm.at[piece(p)], gate_sems.at[p]),
        ]
        for copy in out_copies[-2:]:
            copy.start()
    lax.fori_loop(0, width // LANES, project, 0, unroll=2)
    out_copies += [
        pltpu.make_async_copy(source, target, last_sems.at[n])
        for n, (source, target) in enumerate(
            ((packet_ref, packet_hbm), (state_ref, state_hbm), (inverse_ref, inverse_hbm))
        )
    ]
    for copy in out_copies[-3:]:
        copy.start()
    for copy in out_copies:
        copy.wait()


def near_kernel(
    signal_ref, rates_ref, residue_ref, places_ref, skip_ref, near_ref, mark_ref, out_ref, done_ref, parts_ref
):
    rows = signal_ref.shape[0]
    done_ref[...] = jnp.zeros_like(done_ref)
    size = min(NEAR_GROUP, signal_ref.shape[1])

    def group(i, carry):
        cols = group_of(i, size)
        rates = rates_ref[:, cols]
        nodal = nodal_sum(rates, coefs_of(rates, residue_ref[:, cols]), places_ref[...]).astype(BF16)
        signal = signal_ref[:, cols]
        for k in range(NODES):
            parts_ref[k * rows : (k + 1) * rows] = signal * nodal[k : k + 1]
        out_ref[:, cols] = (
            jnp.dot(near_ref[0], parts_ref[...], preferred_element_type=F32)
            + skip_ref[:, cols] * signal.astype(F32)
        )
        return carry

    lax.fori_loop(0, signal_ref.shape[1] // size, group, 0)


def scan_kernel(rates_ref, gain_ref, taps_ref, packet_ref, mark_ref, enter_ref, done_ref, wide_ref, row_ref, *, rows):
    done_ref[...] = jnp.zeros_like(done_ref)
    count = packet_ref.shape[0]
    first = lax.axis_index("seq") * LANES
    cols = pl.ds(pl.multiple_of(first, LANES), LANES)
    rates = rates_ref[:, cols]
    taps = taps_of(taps_ref, gain_ref, cols)
    for d in range(count):
        wide_ref[d * PACKET : (d + 1) * PACKET] = packet_ref[d].astype(F32)
    x_0, x_1, x_2, x_3, cot_0, cot_1, high, low = [
        wide_ref[pl.ds(EXTRA + n, count, stride=PACKET), :] for n in range(8)
    ]
    scale = high + low
    n_0, n_1, n_2, n_3 = [
        x * jnp.broadcast_to(scale[:, n : n + 1], (count, LANES))
        for n, x in enumerate((x_0, x_1, x_2, x_3))
    ]
    zero = jnp.zeros((1, LANES), F32)

    def before(block):
        return jnp.concatenate([zero, block[:-1]], axis=0)

    def after(block):
        return jnp.concatenate([block[1:], zero], axis=0)

    n_2, n_3 = before(n_2), before(n_3)
    query_0, key_0, value_0 = filtered(taps, n_0, n_3, n_2)
    query_1, key_1, value_1 = filtered(taps, n_1, n_0, n_3)
    heads = (key_0 * value_0, key_1 * value_1, cot_0 * query_0, cot_1 * query_1)
    edges = (before(x_2), before(x_3), after(x_0), after(x_1), after(cot_0), after(cot_1))
    for n, block in enumerate(heads):
        row_ref[n] = block.astype(BF16).astype(F32)
    for n, block in enumerate(edges):
        row_ref[len(heads) + n] = block

    decay = jnp.exp(rates * (-float(rows)))
    lead_0 = jnp.exp(rates * (1.0 - rows))
    lead_1 = jnp.exp(rates * (2.0 - rows))
    decay_1 = jnp.exp(-rates)
    ahead = jnp.zeros((MODES, LANES), F32)
    back = jnp.zeros((MODES, LANES), F32)
    backs = [None] * count
    for d in reversed(range(count)):
        backs[d] = back
        own = wide_ref[d * PACKET + MODES : d * PACKET + 2 * MODES]
        back = decay * back + (own + row_ref[2, d : d + 1] + decay_1 * row_ref[3, d : d + 1])
    for d in range(count):
        extra = [row_ref[len(heads) + n, d : d + 1] for n in range(6)]
        enter_ref[d] = jnp.concatenate([ahead, backs[d]] + extra + [zero, zero], axis=0).astype(BF16)
        own = wide_ref[d * PACKET : d * PACKET + MODES]
        ahead = decay * ahead + (own + lead_0 * row_ref[0, d : d + 1] + lead_1 * row_ref[1, d : d + 1])


def over(block):
    return jnp.sum(block, axis=0, keepdims=True)


def entered_of(enter_ref, i, size, side):
    pieces = size // LANES
    return jnp.concatenate(
        [enter_ref[i * pieces + h, MODES * side : MODES * (side + 1)].astype(F32) for h in range(pieces)], axis=1
    )


def fill_part(
    i, size, x_ref, cot_ref, inverse_ref, gain_ref, taps_ref, rates_ref, residue_ref, skip_ref, places_ref, enter_ref,
    edge_ref, edge_scale, small_ref, nodal_ref, patch_ref, mixed_ref,
):
    cols = group_of(i, size)
    skip = skip_ref[:, cols]
    small_ref[6:8] = edge_ref[0:2, cols] * edge_scale[0:2]
    small_ref[8:16] = x_ref[:, cols].astype(F32)[0:8] * wide(inverse_ref[0:8], size)
    query, key, value = filtered(taps_of(taps_ref, gain_ref, cols), small_ref[8:16], small_ref[7:15], small_ref[6:14])
    mixed = (key * value).astype(BF16).astype(F32)
    gate = (cot_ref[:, cols].astype(F32)[0:8] * query).astype(BF16).astype(F32)
    mixed_ref[:, cols] = mixed
    mixed_0, mixed_1 = mixed[0:1], mixed[1:2]
    gate_0, gate_1 = gate[0:1], gate[1:2]

    rates = rates_ref[:, cols]
    coef = coefs_of(rates, residue_ref[:, cols])
    decay = jnp.exp(-rates)
    rise = jnp.exp(rates)
    now, later, earlier = over(coef), over(coef * decay), over(coef * rise)
    patches = (
        skip * mixed_0 - earlier * mixed_1,
        skip * mixed_1,
        (now + skip) * gate_0 + later * gate_1,
        (now + skip) * gate_1,
    )
    zeros = jnp.zeros((6, size), F32)
    patch_ref[0:8, cols] = jnp.concatenate([patches[0], patches[1], zeros], axis=0)
    patch_ref[8:16, cols] = jnp.concatenate([patches[2], patches[3], zeros], axis=0)

    weights = [
        coef * (decay * entered_of(enter_ref, i, size, 0) + mixed_0 + rise * mixed_1),
        coef * decay * entered_of(enter_ref, i, size, 1),
    ]
    places = wide(places_ref[...], size)
    nodals = [0.0, 0.0]
    for r in range(MODES):
        column = jnp.exp(-rates[r : r + 1] * places)
        nodals = [nodals[side] + column * weights[side][r : r + 1] for side in range(2)]
    for side in range(2):
        high = nodals[side].astype(BF16)
        low = (nodals[side] - high.astype(F32)).astype(BF16)
        nodal_ref[side, :, cols] = jnp.concatenate([high, high, low], axis=0)


def finish_kernel(
    rows, first, count, x_hbm, cot_hbm, ahead_hbm, back_hbm, inverse_ref, gain_ref, taps_ref, spread_ref, enter_ref,
    residue_ref, rates_ref, skip_ref, *refs,
):
    low = first == 0
    if low:
        (
            places_ref, layer_ref, grad_ref, nodal_ref, edge_ref, mixed_ref,
            head_x_ref, head_cot_ref, head_sems, small_ref, patch_ref, *refs,
        ) = refs
    else:
        state_ref, nodal_ref, edge_ref, mixed_ref, layer_ref, grad_ref, *refs = refs
    (
        x_ref, cot_ref, ahead_ref, back_ref, base_ref, normed_refs, one_refs, two_refs, total_ref, load_sems,
    ) = refs
    width = x_ref.shape[1]
    size = normed_refs.shape[2]
    together = normed_refs.shape[0]
    pieces = load_sems.shape[1]
    part = width // pieces
    top = 0 if low else 16
    reach = count + 8 if low else count

    def lanes(p):
        return pl.ds(p * part, part)

    if low:
        heads = [
            pltpu.make_async_copy(source.at[pl.ds(0, 16)], target, head_sems.at[n])
            for n, (source, target) in enumerate(((x_hbm, head_x_ref), (cot_hbm, head_cot_ref)))
        ]
        for copy in heads:
            copy.start()
    loads = []
    for p in range(pieces):
        loads.append([
            pltpu.make_async_copy(
                source.at[pl.ds(lo, target.shape[0]), lanes(p)], target.at[:, lanes(p)], load_sems.at[k, p]
            )
            for k, (source, target, lo) in enumerate((
                (x_hbm, x_ref, first - top),
                (cot_hbm, cot_ref, first),
                (ahead_hbm, ahead_ref, first),
                (back_hbm, back_ref, first),
            ))
        ])
        for copy in loads[p]:
            copy.start()

    total_ref[...] = jnp.zeros_like(total_ref)
    if low:
        def edges(j, total):
            block = enter_ref[j].astype(F32)[EXTRA:PACKET]
            edge_ref[0:8, group_of(j)] = block
            return total + block * block

        total = lax.fori_loop(0, width // LANES, edges, jnp.zeros((8, LANES), F32), unroll=4)
        edge_ref[8:16, 0:LANES] = jnp.broadcast_to(row_scale(total, width), (8, LANES))
        for copy in heads:
            copy.wait()
        fill_size = small_ref.shape[1]
        fill_scale = wide(edge_ref[8:16, 0:LANES], fill_size)

        def fill(i, carry):
            fill_part(
                i, fill_size, head_x_ref, head_cot_ref, inverse_ref, gain_ref, taps_ref, rates_ref, residue_ref,
                skip_ref, places_ref, enter_ref, edge_ref, fill_scale, small_ref, nodal_ref, patch_ref, mixed_ref,
            )
            return carry

        lax.fori_loop(0, width // fill_size, fill, 0)

    edge_scale = wide(edge_ref[8:16, 0:LANES], size)
    inverse = wide(inverse_ref[first : first + reach], size)

    def group(i, normed_ref, one_ref, two_ref):
        cols = group_of(i, size)
        taps = taps_of(taps_ref, gain_ref, cols)
        x = x_ref[top:, cols].astype(F32)[0:reach]
        cot = cot_ref[:, cols].astype(F32)[0:reach]
        normed_ref[16 : reach + 16] = x * inverse
        if low:
            normed_ref[14:16] = edge_ref[0:2, cols] * edge_scale[0:2]
        else:
            above = x_ref[0:16, cols].astype(F32)
            normed_ref[0:16] = above * wide(inverse_ref[first - 16 : first], size)
        now = normed_ref[16 : reach + 16]
        past = normed_ref[15 : reach + 15]
        older = normed_ref[14 : reach + 14]
        query, key, value = filtered(taps, now, past, older)

        convs = []
        for side, near_ref in enumerate((ahead_ref, back_ref)):
            far = jnp.dot(
                spread_ref[side * rows + first : side * rows + first + reach],
                nodal_ref[side, :, cols],
                preferred_element_type=F32,
            )
            total = near_ref[:, cols] + far
            if low:
                total = jnp.concatenate([total[0:8] + patch_ref[8 * side : 8 * side + 8, cols], total[8:]], axis=0)
            convs.append(total.astype(BF16).astype(F32))
        conv, conv_back = convs
        layer_ref[:, cols] = (x[0:count] + query[0:count] * conv[0:count]).astype(BF16)

        grads = (cot * conv, conv_back * value, conv_back * key)
        lagged = [sum(taps[j][i] * grads[j] for j in range(3)) for i in range(3)]
        one_ref[0:reach] = lagged[1]
        two_ref[0:reach] = lagged[2]
        if not low:
            normed_ref[count + 16 : count + 18] = edge_ref[2:4, cols] * edge_scale[2:4]
            n_query, n_key, n_value = filtered(
                taps,
                normed_ref[count + 16 : count + 18],
                normed_ref[count + 15 : count + 17],
                normed_ref[count + 14 : count + 16],
            )
            n_cot = edge_ref[4:6, cols]
            n_mixed = (n_key * n_value).astype(BF16).astype(F32)
            n_gate = (n_cot * n_query).astype(BF16).astype(F32)
            rates = rates_ref[:, cols]
            coef = coefs_of(rates, residue_ref[:, cols])
            decay = jnp.exp(-rates)
            lead = coef * decay
            skip = skip_ref[:, cols]
            entered = [entered_of(enter_ref, i, size, side) for side in range(2)]
            own = (
                state_ref[0:MODES, cols]
                + jnp.exp(rates * (1.0 - rows)) * mixed_ref[0:1, cols]
                + jnp.exp(rates * (2.0 - rows)) * mixed_ref[1:2, cols]
            )
            leave = jnp.exp(rates * (-float(rows))) * entered[0] + own
            direct = over(coef) + skip
            mixed_0, mixed_1 = n_mixed[0:1], n_mixed[1:2]
            gate_0, gate_1 = n_gate[0:1], n_gate[1:2]
            conv_0 = over(lead * leave) + direct * mixed_0
            conv_1 = over(lead * decay * leave) + over(lead) * mixed_0 + direct * mixed_1
            back_0 = over(coef * entered[1]) + skip * gate_0
            back_1 = over(coef * (1.0 / decay) * (entered[1] - gate_0)) + skip * gate_1
            n_conv = jnp.concatenate([conv_0, conv_1], axis=0).astype(BF16).astype(F32)
            n_back = jnp.concatenate([back_0, back_1], axis=0).astype(BF16).astype(F32)
            n_grads = (n_cot * n_conv, n_back * n_value, n_back * n_key)
            one_ref[count : count + 2] = sum(taps[j][1] * n_grads[j] for j in range(3))
            two_ref[count : count + 2] = sum(taps[j][2] * n_grads[j] for j in range(3))
        scaled = lagged[0][0:count] + one_ref[1 : count + 1] + two_ref[2 : count + 2]
        base_ref[:, cols] = cot[0:count] + inverse[0:count] * scaled
        return lane_sums(scaled * x[0:count])

    def groups(i, carry):
        sums = [group(i * together + n, normed_refs.at[n], one_refs.at[n], two_refs.at[n]) for n in range(together)]
        total_ref[...] = total_ref[...] + sum(sums)
        return carry

    for p in range(pieces):
        for copy in loads[p]:
            copy.wait()
        steps = part // size // together
        lax.fori_loop(p * steps, (p + 1) * steps, groups, 0)

    mean = jnp.sum(total_ref[...], axis=1, keepdims=True) * (1.0 / width)
    scale = inverse_ref[first : first + count]
    factor = scale * scale * scale * jnp.broadcast_to(mean, (count, LANES))

    def emit(i, carry):
        cols = group_of(i)
        x = x_ref[top : top + count, cols].astype(F32)
        grad_ref[:, cols] = (base_ref[:, cols] - x * factor).astype(BF16)
        return carry

    lax.fori_loop(0, width // LANES, emit, 0, unroll=4)


def join_kernel(first, layer_ref, grad_ref, *refs):
    layer_hbm, grad_hbm, sems = refs[-3:]
    count = layer_ref.shape[0]
    half = layer_ref.shape[1] // 2
    copies = []
    for n, (source, target) in enumerate(((layer_ref, layer_hbm), (grad_ref, grad_hbm))):
        for h in range(2):
            lanes = pl.ds(h * half, half)
            copies.append(
                pltpu.make_async_copy(source.at[:, lanes], target.at[pl.ds(first, count), lanes], sems.at[n, h])
            )
    for copy in copies:
        copy.start()
    for copy in copies:
        copy.wait()


def shifted(block, axis, distance):
    devices = range(lax.axis_size(axis))
    route = [(i - distance, i) for i in devices if i - distance in devices]
    return lax.ppermute(block, axis, route)


def whole(shape):
    return pl.BlockSpec(shape, lambda *i: (0,) * len(shape))


def across(shape, step, axis=None):
    axis = len(shape) - 1 if axis is None else axis
    block = shape[:axis] + (step,) + shape[axis + 1 :]
    return pl.BlockSpec(block, lambda i: (0,) * axis + (i,) + (0,) * (len(shape) - axis - 1))


def params(mib):
    return pltpu.CompilerParams(vmem_limit_bytes=mib << 20)


def stay(array):
    return pltpu.with_memory_space_constraint(array, pltpu.HBM)


def takes(micros):
    return pl.CostEstimate(
        flops=int(micros * 1.1e9), bytes_accessed=int(micros * 3.5e6), transcendentals=0
    )


def start_call(x, cot, gain, taps, rates, moments):
    rows, width = x.shape
    pieces = PIECES
    far = pl.BlockSpec(memory_space=pltpu.HBM)
    outs = [
        (x.shape, BF16),
        (x.shape, BF16),
        ((width // LANES, PACKET, LANES), BF16),
        ((2 * MODES, width), F32),
        ((rows, LANES), F32),
    ]
    ins = (x, cot, gain, taps, rates, moments)
    held = (x, cot, gain, taps, rates, moments)
    return pl.pallas_call(
        functools.partial(start_kernel, [float(p) for p in node_places(rows)]),
        in_specs=[far] * len(ins),
        out_specs=[far] * len(outs),
        out_shape=[pltpu.HBM(*out) for out in outs],
        scratch_shapes=[pltpu.VMEM(array.shape, array.dtype) for array in held]
        + [pltpu.VMEM(*out) for out in outs]
        + [
            pltpu.VMEM((rows + 8, min(START_GROUP, width // pieces)), F32),
            pltpu.VMEM((2 * PADDED, width), F32),
            pltpu.SemaphoreType.DMA((pieces,)),
            pltpu.SemaphoreType.DMA((pieces,)),
            pltpu.SemaphoreType.DMA((4,)),
            pltpu.SemaphoreType.DMA((pieces,)),
            pltpu.SemaphoreType.DMA((pieces,)),
            pltpu.SemaphoreType.DMA((3,)),
        ],
        compiler_params=params(24),
        cost_estimate=takes(6),
        name="start",
    )(*[stay(array) for array in ins])


def near_call(side, signal, rates, residue, places, skip, near, mark):
    rows, width = signal.shape
    step = min(NEAR_STEP, width)
    return pl.pallas_call(
        near_kernel,
        grid=(width // step,),
        in_specs=[
            across(signal.shape, step),
            across(rates.shape, step), across(rates.shape, step), whole(places.shape),
            across(skip.shape, step),
            pl.BlockSpec((1,) + near.shape[1:], lambda i: (side, 0, 0)),
            whole((8, LANES)),
        ],
        out_specs=[across(signal.shape, step), whole((8, LANES))],
        out_shape=[pltpu.HBM(signal.shape, F32), shape((8, LANES), F32)],
        scratch_shapes=[pltpu.VMEM((NODES * rows, min(NEAR_GROUP, width)), BF16)],
        compiler_params=params(16),
        cost_estimate=takes(4),
        name="near",
    )(stay(signal), rates, residue, places, skip, stay(near), mark)


def scan_call(rates, gain, taps, gathered, mark, rows):
    return pl.pallas_call(
        functools.partial(scan_kernel, rows=rows),
        out_shape=[shape(gathered.shape, BF16), shape((8, LANES), F32)],
        scratch_shapes=[
            pltpu.VMEM((gathered.shape[0] * PACKET, LANES), F32),
            pltpu.VMEM((10, gathered.shape[0], LANES), F32),
        ],
        compiler_params=params(6),
        cost_estimate=takes(1),
        name="scan",
    )(rates, gain, taps, gathered, mark)


def finish_call(rows, first, count, *arrays):
    x = arrays[0]
    width = x.shape[1]
    low = first == 0
    pieces = PIECES
    size = min(FINISH_GROUP, width)
    together = min(FINISH_TOGETHER, width // pieces // size)
    fill_size = min(FILL_GROUP, width)
    far = pl.BlockSpec(memory_space=pltpu.HBM)
    near = pl.BlockSpec(memory_space=pltpu.VMEM)
    half = shape((count, width), BF16)
    out_shape = [half, half]
    scratch = []
    above, below, reach = (0, 16, count + 8) if low else (16, 0, count)
    if low:
        out_shape += [shape((2, 3 * PADDED, width), BF16), shape((16, width), F32), shape((8, width), F32)]
        scratch = [
            pltpu.VMEM((16, width), BF16),
            pltpu.VMEM((16, width), BF16),
            pltpu.SemaphoreType.DMA((2,)),
            pltpu.VMEM((16, fill_size), F32),
            pltpu.VMEM((16, width), F32),
        ]
    return pl.pallas_call(
        functools.partial(finish_kernel, rows, first, count),
        in_specs=[far] * 4 + [near] * (len(arrays) - 4),
        out_specs=[near] * len(out_shape),
        out_shape=out_shape,
        scratch_shapes=scratch
        + [
            pltpu.VMEM((above + count + below, width), BF16),
            pltpu.VMEM((count + below, width), BF16),
            pltpu.VMEM((reach, width), F32),
            pltpu.VMEM((reach, width), F32),
            pltpu.VMEM((count, width), F32),
            pltpu.VMEM((together, reach + 24, size), F32),
            pltpu.VMEM((together, reach + 8, size), F32),
            pltpu.VMEM((together, reach + 8, size), F32),
            pltpu.VMEM((count, LANES), F32),
            pltpu.SemaphoreType.DMA((4, pieces)),
        ],
        compiler_params=params(24),
        cost_estimate=takes(6),
        name="finish",
    )(*[stay(array) for array in arrays[:4]], *arrays[4:])


def join_call(rows, first, layer, grad, *wholes):
    far = pl.BlockSpec(memory_space=pltpu.HBM)
    near = pl.BlockSpec(memory_space=pltpu.VMEM)
    out = shape((rows, layer.shape[1]), BF16)
    return pl.pallas_call(
        functools.partial(join_kernel, first),
        in_specs=[near, near] + [far] * len(wholes),
        out_specs=[far, far],
        out_shape=[out, out],
        scratch_shapes=[pltpu.SemaphoreType.DMA((2, 2))],
        input_output_aliases={2 + n: n for n in range(len(wholes))},
        compiler_params=params(4),
        cost_estimate=takes(1),
        name="join",
    )(layer, grad, *wholes)


def local(section_input, cotangent, norm_gain, short_filter, decay_rate, residue, skip_gain):
    x = section_input[0]
    cot = cotangent[0]
    rows = x.shape[0]
    taps = jnp.transpose(short_filter, (1, 2, 0, 3))
    rates = decay_rate[0]
    fixed = {name: jnp.asarray(table) for name, table in constants(rows).items()}

    weights = residue[0]
    mixed, gate, packet, state, inverse = start_call(x, cot, norm_gain, taps, rates, fixed["moments"])
    gathered = lax.all_to_all(packet, "seq", split_axis=0, concat_axis=0, tiled=True)
    near = (rates, weights, fixed["places"], skip_gain, fixed["near"])
    ahead, mark = near_call(0, mixed, *near, stay(inverse))
    entering, mark = scan_call(rates, norm_gain, taps, gathered, mark, rows)
    enter = lax.all_to_all(entering, "seq", split_axis=0, concat_axis=0, tiled=True)
    back, mark = near_call(1, gate, *near, mark)

    common = (x, cot, ahead, back, inverse, norm_gain, taps, fixed["spread"], enter, weights, rates, skip_gain)
    layer, grad, *passed = finish_call(rows, 0, SPLIT, *common, fixed["places"])
    on_low = shifted(layer, "section", 1)
    back_low = shifted(grad, "section", -1)
    layer, grad = finish_call(rows, SPLIT, rows - SPLIT, *common, state, *passed)
    on_high = shifted(layer, "section", 1)
    back_high = shifted(grad, "section", -1)
    joined = join_call(rows, 0, on_low, back_low)
    passed_on, passed_back = join_call(rows, SPLIT, on_high, back_high, *joined)
    return passed_on[None], passed_back[None]


def solution(mesh):
    in_specs = (
        P("section", "seq", None),
        P("section", "seq", None),
        P("section", None),
        P("section", None, None, None),
        P("section", None, None),
        P("section", None, None),
        P("section", None),
    )
    out_specs = (P("section", "seq", None), P("section", "seq", None))
    return jax.shard_map(local, mesh=mesh, in_specs=in_specs, out_specs=out_specs, check_vma=False)
```

```python
import functools

import jax
import jax.numpy as jnp
import ml_dtypes
import numpy as np
from jax import lax
from jax.experimental import pallas as pl
from jax.experimental.pallas import tpu as pltpu
from jax.sharding import PartitionSpec as P

MODES = 16
NODES = 14
PADDED = 16
PACKET = 40
EXTRA = 32
LANES = 128
START_GROUP = 128
START_TOGETHER = 8
PROJECT_UNROLL = 4
PIECES = 4
SPLIT = 80
NEAR_STEP = 1024
NEAR_GROUP = 1024
FINISH_GROUP = 128
FINISH_TOGETHER = 8
F32 = jnp.float32
BF16 = jnp.bfloat16
shape = jax.ShapeDtypeStruct


def node_places(rows):
    k = np.arange(NODES)
    return 0.5 * (rows - 1) * (1.0 - np.cos((2 * k + 1) * np.pi / (2 * NODES)))


def cardinals(rows):
    nodes = node_places(rows)
    lags = np.arange(rows, dtype=np.float64)
    table = np.ones((rows, NODES))
    for k in range(NODES):
        for m in range(NODES):
            if m != k:
                table[:, k] *= (lags - nodes[m]) / (nodes[k] - nodes[m])
    return table


def halves(table):
    high = table.astype(ml_dtypes.bfloat16)
    low = (table - high.astype(np.float64)).astype(ml_dtypes.bfloat16)
    return high, low


def constants(rows):
    table = cardinals(rows)
    padded = np.zeros((rows, PADDED))
    padded[:, :NODES] = table
    high, low = halves(padded)
    flip_high, flip_low = high[::-1], low[::-1]
    moment_ahead = np.concatenate([flip_high.T, flip_low.T], axis=0)
    moment_back = np.concatenate([high.T, low.T], axis=0)
    first_rows = np.zeros((rows, PADDED), high.dtype)
    first_rows[0, NODES] = first_rows[1, NODES + 1] = 1.0
    spread_ahead = np.concatenate([high + first_rows, low], axis=1)
    spread_back = np.concatenate([flip_high + first_rows, flip_low], axis=1)
    lag = np.arange(rows)[:, None] - np.arange(rows)[None, :]
    toeplitz = np.where(lag[:, :, None] >= 0, table[np.maximum(lag, 0)], 0.0)
    near_ahead = np.transpose(toeplitz, (0, 2, 1)).reshape(rows, NODES * rows)
    near_back = np.transpose(toeplitz, (1, 2, 0)).reshape(rows, NODES * rows)
    places = np.zeros((PADDED, LANES), np.float32)
    places[:NODES] = node_places(rows)[:, None]
    cast = ml_dtypes.bfloat16
    return dict(
        moments=np.concatenate(
            [
                np.concatenate([moment_ahead, np.zeros_like(moment_ahead)], axis=1),
                np.concatenate([np.zeros_like(moment_back), moment_back], axis=1),
            ],
            axis=0,
        ),
        spread=np.concatenate([spread_ahead, spread_back], axis=0),
        near=np.stack([near_ahead, near_back]).astype(cast),
        places=places,
    )


def coefs_of(rates, residue):
    return residue * jnp.sqrt(1.0 - jnp.exp(-2.0 * rates))


def nodal_sum(rates, weight, places):
    places = wide(places, rates.shape[1])
    total = jnp.exp(-rates[0:1] * places) * weight[0:1]
    for r in range(1, MODES):
        total = total + jnp.exp(-rates[r : r + 1] * places) * weight[r : r + 1]
    return total


def taps_of(taps_ref, gain_ref, cols):
    gain = gain_ref[:, cols]
    return [[taps_ref[j, i, :, cols] * gain for i in range(3)] for j in range(3)]


def group_of(index, size=LANES):
    return pl.ds(pl.multiple_of(index * size, size), size)


def wide(block, width):
    return jnp.concatenate([block] * (width // LANES), axis=1)


def row_scale(block_sum, width):
    return lax.rsqrt(jnp.sum(block_sum, axis=1, keepdims=True) * (1.0 / width) + 1e-06)


def lane_sums(block):
    total = block[:, :LANES]
    for i in range(1, block.shape[1] // LANES):
        total = total + block[:, i * LANES : (i + 1) * LANES]
    return total


def filtered(taps, now, past, older):
    return [t[0] * now + t[1] * past + t[2] * older for t in taps]


def start_kernel(
    nodes, x_hbm, cot_hbm, gain_hbm, taps_hbm, rates_hbm, moments_hbm,
    mixed_hbm, gate_hbm, packet_hbm, inverse_hbm,
    x_ref, cot_ref, gain_ref, taps_ref, rates_ref, moments_ref, mixed_ref, gate_ref, packet_ref, inverse_ref,
    normed_refs, moment_ref, x_sems, cot_sems, table_sems, mixed_sems, gate_sems, last_sems,
):
    rows, width = x_ref.shape
    size = normed_refs.shape[2]
    pieces = x_sems.shape[0]
    part = width // pieces

    def piece(p):
        return slice(None), pl.ds(p * part, part)

    x_copies = [pltpu.make_async_copy(x_hbm.at[piece(p)], x_ref.at[piece(p)], x_sems.at[p]) for p in range(pieces)]
    cot_copies = [
        pltpu.make_async_copy(cot_hbm.at[piece(p)], cot_ref.at[piece(p)], cot_sems.at[p]) for p in range(pieces)
    ]
    table_copies = [
        pltpu.make_async_copy(source, target, table_sems.at[n])
        for n, (source, target) in enumerate(
            ((gain_hbm, gain_ref), (taps_hbm, taps_ref), (moments_hbm, moments_ref), (rates_hbm, rates_ref))
        )
    ]
    for copy in x_copies + table_copies + cot_copies:
        copy.start()

    for n in range(normed_refs.shape[0]):
        normed_refs[n, 0:8] = jnp.zeros((8, size), F32)
    total = jnp.zeros((rows, LANES), F32)
    for p in range(pieces):
        x_copies[p].wait()

        def square(i, total):
            x = x_ref[:, group_of(p * (part // LANES) + i)].astype(F32)
            return total + x * x

        total = lax.fori_loop(0, part // LANES, square, total, unroll=4)
    inverse_ref[...] = jnp.broadcast_to(row_scale(total, width), (rows, LANES))
    for copy in table_copies:
        copy.wait()

    lane = lax.broadcasted_iota(jnp.int32, (1, LANES), 1)
    scale = jnp.zeros((1, LANES), F32)
    for n, row in enumerate((0, 1, rows - 2, rows - 1)):
        scale = jnp.where(lane == n, inverse_ref[row : row + 1], scale)
    scale_high = scale.astype(BF16).astype(F32)
    scales = jnp.concatenate([scale_high, scale - scale_high], axis=0)

    def group(i, normed_ref):
        cols = group_of(i, size)
        now = x_ref[:, cols].astype(F32) * wide(inverse_ref[...], size)
        normed_ref[8 : rows + 8] = now
        past = normed_ref[7 : rows + 7]
        older = normed_ref[6 : rows + 6]
        query, key, value = filtered(taps_of(taps_ref, gain_ref, cols), now, past, older)
        kept = lax.broadcasted_iota(jnp.int32, (16, size), 0) >= 2
        for signal, out_ref in ((key * value, mixed_ref), (cot_ref[:, cols].astype(F32) * query, gate_ref)):
            head = jnp.where(kept, signal[0:16], 0.0)
            out_ref[:, cols] = jnp.concatenate([head, signal[16:]], axis=0).astype(BF16)

    together = normed_refs.shape[0]

    def groups(i, carry):
        for n in range(together):
            group(i * together + n, normed_refs.at[n])
        return carry

    def gather(p):
        cols = pl.ds(p * part, part)
        signals = jnp.concatenate([mixed_ref[:, cols], gate_ref[:, cols]], axis=0)
        both = jnp.dot(moments_ref[...], signals, preferred_element_type=F32)
        for side in range(2):
            high = 2 * PADDED * side
            moment_ref[PADDED * side : PADDED * (side + 1), cols] = (
                both[high : high + PADDED] + both[high + PADDED : high + 2 * PADDED]
            )

    def project(i, carry):
        cols = group_of(i)
        rates = rates_ref[:, cols]
        states = [0.0, 0.0]
        for k in range(NODES):
            power = jnp.exp(rates * (-nodes[k]))
            states = [
                states[side] + power * moment_ref[PADDED * side + k : PADDED * side + k + 1, cols]
                for side in range(2)
            ]
        x_head = x_ref[0:16, cols].astype(F32)
        x_tail = x_ref[rows - 16 : rows, cols].astype(F32)
        cot_head = cot_ref[0:16, cols].astype(F32)
        packet_ref[i] = jnp.concatenate(
            states + [x_head[0:2], x_tail[14:16], cot_head[0:2], scales], axis=0
        ).astype(BF16)
        return carry

    out_copies = []
    for p in range(pieces):
        cot_copies[p].wait()
        steps = part // size // together
        lax.fori_loop(p * steps, (p + 1) * steps, groups, 0)
        out_copies += [
            pltpu.make_async_copy(mixed_ref.at[piece(p)], mixed_hbm.at[piece(p)], mixed_sems.at[p]),
            pltpu.make_async_copy(gate_ref.at[piece(p)], gate_hbm.at[piece(p)], gate_sems.at[p]),
        ]
        for copy in out_copies[-2:]:
            copy.start()
        gather(p)
        lax.fori_loop(p * (part // LANES), (p + 1) * (part // LANES), project, 0, unroll=PROJECT_UNROLL)
    out_copies += [
        pltpu.make_async_copy(source, target, last_sems.at[n])
        for n, (source, target) in enumerate(
            ((packet_ref, packet_hbm), (inverse_ref, inverse_hbm))
        )
    ]
    for copy in out_copies[-2:]:
        copy.start()
    for copy in out_copies:
        copy.wait()


def near_kernel(
    signal_ref, rates_ref, residue_ref, places_ref, skip_ref, near_ref, mark_ref, out_ref, done_ref, parts_ref
):
    rows = signal_ref.shape[0]
    done_ref[...] = jnp.zeros_like(done_ref)
    size = min(NEAR_GROUP, signal_ref.shape[1])

    def group(i, carry):
        cols = group_of(i, size)
        rates = rates_ref[:, cols]
        nodal = nodal_sum(rates, coefs_of(rates, residue_ref[:, cols]), places_ref[...])
        signal = signal_ref[:, cols].astype(F32)
        for k in range(NODES):
            parts_ref[k * rows : (k + 1) * rows] = (signal * nodal[k : k + 1]).astype(BF16)
        out_ref[:, cols] = (
            jnp.dot(near_ref[0], parts_ref[...], preferred_element_type=F32)
            + skip_ref[:, cols] * signal
        )
        return carry

    lax.fori_loop(0, signal_ref.shape[1] // size, group, 0)


def over(block):
    return jnp.sum(block, axis=0, keepdims=True)


def scan_kernel(
    rates_ref, residue_ref, skip_ref, gain_ref, taps_ref, places_ref, packet_ref, mark_ref, enter_ref, done_ref,
    wide_ref, row_ref, base_ref, column_ref, *, rows,
):
    done_ref[...] = jnp.zeros_like(done_ref)
    count = packet_ref.shape[0]
    cols = pl.ds(pl.multiple_of(lax.axis_index("seq") * LANES, LANES), LANES)
    rates = rates_ref[:, cols]
    skip = skip_ref[:, cols]
    taps = taps_of(taps_ref, gain_ref, cols)
    coef = coefs_of(rates, residue_ref[:, cols])
    fall = jnp.exp(-rates)
    rise = jnp.exp(rates)
    now, later, earlier = over(coef), over(coef * fall), over(coef * rise)
    places = places_ref[...]
    for r in range(MODES):
        column_ref[r] = jnp.exp(-rates[r : r + 1] * places)
    for d in range(count):
        wide_ref[d * PACKET : (d + 1) * PACKET] = packet_ref[d].astype(F32)
    x_0, x_1, x_2, x_3, cot_0, cot_1, high, low = [
        wide_ref[pl.ds(EXTRA + n, count, stride=PACKET), :] for n in range(8)
    ]
    scale = high + low
    n_0, n_1, n_2, n_3 = [
        x * jnp.broadcast_to(scale[:, n : n + 1], (count, LANES)) for n, x in enumerate((x_0, x_1, x_2, x_3))
    ]
    zero = jnp.zeros((1, LANES), F32)

    def before(block):
        return jnp.concatenate([zero, block[:-1]], axis=0)

    def after(block):
        return jnp.concatenate([block[1:], zero], axis=0)

    n_2, n_3 = before(n_2), before(n_3)
    query_0, key_0, value_0 = filtered(taps, n_0, n_3, n_2)
    query_1, key_1, value_1 = filtered(taps, n_1, n_0, n_3)
    mixed_0, mixed_1, gate_0, gate_1 = [
        block.astype(BF16).astype(F32)
        for block in (key_0 * value_0, key_1 * value_1, cot_0 * query_0, cot_1 * query_1)
    ]
    rows_kept = (
        mixed_0,
        mixed_1,
        gate_0,
        gate_1,
        skip * mixed_0 - earlier * mixed_1,
        skip * mixed_1,
        (now + skip) * gate_0 + later * gate_1,
        (now + skip) * gate_1,
    )
    for n, block in enumerate(rows_kept):
        row_ref[n] = block

    decay = jnp.exp(rates * (-float(rows)))
    lead_0 = jnp.exp(rates * (1.0 - rows))
    lead_1 = jnp.exp(rates * (2.0 - rows))

    def spread(weight):
        total = column_ref[0] * weight[0:1]
        for r in range(1, MODES):
            total = total + column_ref[r] * weight[r : r + 1]
        return total[0:NODES]

    ahead = jnp.zeros((MODES, LANES), F32)
    back = jnp.zeros((MODES, LANES), F32)
    for step in range(count):
        d = step
        reached = coef * fall * ahead
        base_ref[0, d : d + 1] = over(reached)
        base_ref[1, d : d + 1] = over(reached * fall)
        nodal = spread(reached + coef * (row_ref[0, d : d + 1] + rise * row_ref[1, d : d + 1]))
        own = wide_ref[d * PACKET : d * PACKET + MODES]
        wide_ref[d * PACKET : d * PACKET + PADDED] = jnp.concatenate(
            [nodal, row_ref[4, d : d + 1], row_ref[5, d : d + 1]], axis=0
        )
        ahead = decay * ahead + (own + lead_0 * row_ref[0, d : d + 1] + lead_1 * row_ref[1, d : d + 1])

        d = count - 1 - step
        nodal = spread(coef * fall * back)
        back = decay * back + wide_ref[d * PACKET + MODES : d * PACKET + 2 * MODES]
        wide_ref[d * PACKET + PADDED : d * PACKET + 2 * PADDED] = jnp.concatenate(
            [nodal, row_ref[6, d : d + 1], row_ref[7, d : d + 1]], axis=0
        )
        reached = coef * back
        base_ref[2, d : d + 1] = over(reached)
        base_ref[3, d : d + 1] = over(reached * rise)
        back = back + row_ref[2, d : d + 1] + fall * row_ref[3, d : d + 1]

    conv_0 = base_ref[0] + (now + skip) * mixed_0
    conv_1 = base_ref[1] + later * mixed_0 + (now + skip) * mixed_1
    back_0 = base_ref[2] + row_ref[6]
    back_1 = base_ref[3] + row_ref[7]
    conv_0, conv_1, back_0, back_1 = [block.astype(BF16).astype(F32) for block in (conv_0, conv_1, back_0, back_1)]
    grads_0 = (cot_0 * conv_0, back_0 * value_0, back_0 * key_0)
    grads_1 = (cot_1 * conv_1, back_1 * value_1, back_1 * key_1)
    edges = (
        before(x_2),
        before(x_3),
        after(sum(taps[j][1] * grads_0[j] for j in range(3))),
        after(sum(taps[j][2] * grads_0[j] for j in range(3))),
        after(sum(taps[j][2] * grads_1[j] for j in range(3))),
    )
    for n, block in enumerate(edges):
        row_ref[n] = block
    unused = jnp.zeros((PACKET - EXTRA - len(edges), LANES), F32)
    for d in range(count):
        extra = [row_ref[n, d : d + 1] for n in range(len(edges))]
        wide_ref[d * PACKET + EXTRA : (d + 1) * PACKET] = jnp.concatenate(extra + [unused], axis=0)
        enter_ref[d] = wide_ref[d * PACKET : (d + 1) * PACKET].astype(BF16)


def finish_kernel(
    rows, first, count, x_hbm, cot_hbm, ahead_hbm, back_hbm, inverse_ref, gain_ref, taps_ref, spread_ref, enter_ref,
    *refs,
):
    low = first == 0
    if low:
        layer_ref, grad_ref, edge_ref, *refs = refs
    else:
        edge_ref, layer_ref, grad_ref, *refs = refs
    (
        x_ref, cot_ref, ahead_ref, back_ref, base_ref, normed_refs, one_refs, two_refs, total_ref, load_sems,
    ) = refs
    width = x_ref.shape[1]
    size = normed_refs.shape[2]
    together = normed_refs.shape[0]
    pieces = load_sems.shape[1]
    part = width // pieces
    top = 0 if low else 16
    reach = count + 8 if low else count

    def lanes(p):
        return pl.ds(p * part, part)

    loads = []
    for p in range(pieces):
        loads.append([
            pltpu.make_async_copy(
                source.at[pl.ds(lo, target.shape[0]), lanes(p)], target.at[:, lanes(p)], load_sems.at[k, p]
            )
            for k, (source, target, lo) in enumerate((
                (x_hbm, x_ref, first - top),
                (cot_hbm, cot_ref, first),
                (ahead_hbm, ahead_ref, first),
                (back_hbm, back_ref, first),
            ))
        ])
        for copy in loads[p]:
            copy.start()

    total_ref[...] = jnp.zeros_like(total_ref)
    if low:
        def edges(j, total):
            block = enter_ref[j].astype(F32)[EXTRA:PACKET]
            edge_ref[0:8, group_of(j)] = block
            return total + block * block

        total = lax.fori_loop(0, width // LANES, edges, jnp.zeros((8, LANES), F32), unroll=4)
        edge_ref[8:16, 0:LANES] = jnp.broadcast_to(row_scale(total, width), (8, LANES))

    edge_scale = wide(edge_ref[8:16, 0:LANES], size)
    inverse = wide(inverse_ref[first : first + reach], size)
    blocks = size // LANES

    def group(i, normed_ref, one_ref, two_ref):
        cols = group_of(i, size)
        taps = taps_of(taps_ref, gain_ref, cols)
        x = x_ref[top:, cols].astype(F32)[0:reach]
        cot = cot_ref[:, cols].astype(F32)[0:reach]
        normed_ref[16 : reach + 16] = x * inverse
        if low:
            normed_ref[14:16] = edge_ref[0:2, cols] * edge_scale[0:2]
        else:
            above = x_ref[0:16, cols].astype(F32)
            normed_ref[0:16] = above * wide(inverse_ref[first - 16 : first], size)
        now = normed_ref[16 : reach + 16]
        past = normed_ref[15 : reach + 15]
        older = normed_ref[14 : reach + 14]
        query, key, value = filtered(taps, now, past, older)

        convs = []
        for side, near_ref in enumerate((ahead_ref, back_ref)):
            nodal = jnp.concatenate(
                [enter_ref[i * blocks + h, PADDED * side : PADDED * (side + 1)] for h in range(blocks)], axis=1
            )
            far = jnp.dot(
                spread_ref[side * rows + first : side * rows + first + cot_ref.shape[0]],
                jnp.concatenate([nodal, nodal], axis=0),
                preferred_element_type=F32,
            )
            total = near_ref[:, cols] + far[0:reach]
            convs.append(total.astype(BF16).astype(F32))
        conv, conv_back = convs
        layer_ref[:, cols] = (x[0:count] + query[0:count] * conv[0:count]).astype(BF16)

        grads = (cot * conv, conv_back * value, conv_back * key)
        lagged = [sum(taps[j][i] * grads[j] for j in range(3)) for i in range(3)]
        one_ref[0:reach] = lagged[1]
        two_ref[0:reach] = lagged[2]
        if not low:
            one_ref[count : count + 1] = edge_ref[2:3, cols]
            two_ref[count : count + 2] = edge_ref[3:5, cols]
        scaled = lagged[0][0:count] + one_ref[1 : count + 1] + two_ref[2 : count + 2]
        base_ref[:, cols] = cot[0:count] + inverse[0:count] * scaled
        return lane_sums(scaled * x[0:count])

    def groups(i, carry):
        sums = [group(i * together + n, normed_refs.at[n], one_refs.at[n], two_refs.at[n]) for n in range(together)]
        total_ref[...] = total_ref[...] + sum(sums)
        return carry

    for p in range(pieces):
        for copy in loads[p]:
            copy.wait()
        steps = part // size // together
        lax.fori_loop(p * steps, (p + 1) * steps, groups, 0)

    mean = jnp.sum(total_ref[...], axis=1, keepdims=True) * (1.0 / width)
    scale = inverse_ref[first : first + count]
    factor = scale * scale * scale * jnp.broadcast_to(mean, (count, LANES))

    def emit(i, carry):
        cols = group_of(i)
        x = x_ref[top : top + count, cols].astype(F32)
        grad_ref[:, cols] = (base_ref[:, cols] - x * factor).astype(BF16)
        return carry

    lax.fori_loop(0, width // LANES, emit, 0, unroll=4)


def join_kernel(first, layer_ref, grad_ref, *refs):
    layer_hbm, grad_hbm, sems = refs[-3:]
    count = layer_ref.shape[0]
    half = layer_ref.shape[1] // 2
    copies = []
    for n, (source, target) in enumerate(((layer_ref, layer_hbm), (grad_ref, grad_hbm))):
        for h in range(2):
            lanes = pl.ds(h * half, half)
            copies.append(
                pltpu.make_async_copy(source.at[:, lanes], target.at[pl.ds(first, count), lanes], sems.at[n, h])
            )
    for copy in copies:
        copy.start()
    for copy in copies:
        copy.wait()


def shifted(block, axis, distance):
    devices = range(lax.axis_size(axis))
    route = [(i - distance, i) for i in devices if i - distance in devices]
    return lax.ppermute(block, axis, route)


def whole(shape):
    return pl.BlockSpec(shape, lambda *i: (0,) * len(shape))


def across(shape, step, axis=None):
    axis = len(shape) - 1 if axis is None else axis
    block = shape[:axis] + (step,) + shape[axis + 1 :]
    return pl.BlockSpec(block, lambda i: (0,) * axis + (i,) + (0,) * (len(shape) - axis - 1))


def params(mib):
    return pltpu.CompilerParams(vmem_limit_bytes=mib << 20)


def stay(array):
    return pltpu.with_memory_space_constraint(array, pltpu.HBM)


def takes(micros):
    return pl.CostEstimate(
        flops=int(micros * 1.1e9), bytes_accessed=int(micros * 3.5e6), transcendentals=0
    )


def start_call(x, cot, gain, taps, rates, moments):
    rows, width = x.shape
    pieces = PIECES
    far = pl.BlockSpec(memory_space=pltpu.HBM)
    outs = [
        (x.shape, BF16),
        (x.shape, BF16),
        ((width // LANES, PACKET, LANES), BF16),
        ((rows, LANES), F32),
    ]
    ins = (x, cot, gain, taps, rates, moments)
    held = (x, cot, gain, taps, rates, moments)
    return pl.pallas_call(
        functools.partial(start_kernel, [float(p) for p in node_places(rows)]),
        in_specs=[far] * len(ins),
        out_specs=[far] * len(outs),
        out_shape=[pltpu.HBM(*out) for out in outs],
        scratch_shapes=[pltpu.VMEM(array.shape, array.dtype) for array in held]
        + [pltpu.VMEM(*out) for out in outs]
        + [
            pltpu.VMEM((min(START_TOGETHER, width // pieces // START_GROUP), rows + 8, START_GROUP), F32),
            pltpu.VMEM((2 * PADDED, width), F32),
            pltpu.SemaphoreType.DMA((pieces,)),
            pltpu.SemaphoreType.DMA((pieces,)),
            pltpu.SemaphoreType.DMA((4,)),
            pltpu.SemaphoreType.DMA((pieces,)),
            pltpu.SemaphoreType.DMA((pieces,)),
            pltpu.SemaphoreType.DMA((2,)),
        ],
        compiler_params=params(24),
        cost_estimate=takes(6),
        name="start",
    )(*[stay(array) for array in ins])


def near_call(side, signal, rates, residue, places, skip, near, mark):
    rows, width = signal.shape
    step = min(NEAR_STEP, width)
    return pl.pallas_call(
        near_kernel,
        grid=(width // step,),
        in_specs=[
            across(signal.shape, step),
            across(rates.shape, step), across(rates.shape, step), whole(places.shape),
            across(skip.shape, step),
            pl.BlockSpec((1,) + near.shape[1:], lambda i: (side, 0, 0)),
            whole((8, LANES)),
        ],
        out_specs=[across(signal.shape, step), whole((8, LANES))],
        out_shape=[pltpu.HBM(signal.shape, F32), shape((8, LANES), F32)],
        scratch_shapes=[pltpu.VMEM((NODES * rows, min(NEAR_GROUP, width)), BF16)],
        compiler_params=params(16),
        cost_estimate=takes(4),
        name="near",
    )(stay(signal), rates, residue, places, skip, stay(near), mark)


def scan_call(rates, residue, skip, gain, taps, places, gathered, mark, rows):
    count = gathered.shape[0]
    return pl.pallas_call(
        functools.partial(scan_kernel, rows=rows),
        out_shape=[shape(gathered.shape, BF16), shape((8, LANES), F32)],
        scratch_shapes=[
            pltpu.VMEM((count * PACKET, LANES), F32),
            pltpu.VMEM((8, count, LANES), F32),
            pltpu.VMEM((4, count, LANES), F32),
            pltpu.VMEM((MODES, PADDED, LANES), F32),
        ],
        compiler_params=params(8),
        cost_estimate=takes(2),
        name="scan",
    )(rates, residue, skip, gain, taps, places, gathered, mark)


def finish_call(rows, first, count, *arrays):
    x = arrays[0]
    width = x.shape[1]
    low = first == 0
    pieces = PIECES
    size = min(FINISH_GROUP, width)
    together = min(FINISH_TOGETHER, width // pieces // size)
    far = pl.BlockSpec(memory_space=pltpu.HBM)
    near = pl.BlockSpec(memory_space=pltpu.VMEM)
    half = shape((count, width), BF16)
    out_shape = [half, half]
    above, below, reach = (0, 16, count + 8) if low else (16, 0, count)
    if low:
        out_shape += [shape((16, width), F32)]
    return pl.pallas_call(
        functools.partial(finish_kernel, rows, first, count),
        in_specs=[far] * 4 + [near] * (len(arrays) - 4),
        out_specs=[near] * len(out_shape),
        out_shape=out_shape,
        scratch_shapes=[
            pltpu.VMEM((above + count + below, width), BF16),
            pltpu.VMEM((count + below, width), BF16),
            pltpu.VMEM((reach, width), F32),
            pltpu.VMEM((reach, width), F32),
            pltpu.VMEM((count, width), F32),
            pltpu.VMEM((together, reach + 24, size), F32),
            pltpu.VMEM((together, reach + 8, size), F32),
            pltpu.VMEM((together, reach + 8, size), F32),
            pltpu.VMEM((count, LANES), F32),
            pltpu.SemaphoreType.DMA((4, pieces)),
        ],
        compiler_params=params(24),
        cost_estimate=takes(6),
        name="finish",
    )(*[stay(array) for array in arrays[:4]], *arrays[4:])


def join_call(rows, first, layer, grad, *wholes):
    far = pl.BlockSpec(memory_space=pltpu.HBM)
    near = pl.BlockSpec(memory_space=pltpu.VMEM)
    out = shape((rows, layer.shape[1]), BF16)
    return pl.pallas_call(
        functools.partial(join_kernel, first),
        in_specs=[near, near] + [far] * len(wholes),
        out_specs=[far, far],
        out_shape=[out, out],
        scratch_shapes=[pltpu.SemaphoreType.DMA((2, 2))],
        input_output_aliases={2 + n: n for n in range(len(wholes))},
        compiler_params=params(4),
        cost_estimate=takes(1),
        name="join",
    )(layer, grad, *wholes)


def local(section_input, cotangent, norm_gain, short_filter, decay_rate, residue, skip_gain):
    x = section_input[0]
    cot = cotangent[0]
    rows = x.shape[0]
    taps = jnp.transpose(short_filter, (1, 2, 0, 3))
    rates = decay_rate[0]
    fixed = {name: jnp.asarray(table) for name, table in constants(rows).items()}

    weights = residue[0]
    mixed, gate, packet, inverse = start_call(x, cot, norm_gain, taps, rates, fixed["moments"])
    gathered = lax.all_to_all(packet, "seq", split_axis=0, concat_axis=0, tiled=True)
    near = (rates, weights, fixed["places"], skip_gain, fixed["near"])
    ahead, mark = near_call(0, mixed, *near, stay(inverse))
    entering, mark = scan_call(rates, weights, skip_gain, norm_gain, taps, fixed["places"], gathered, mark, rows)
    enter = lax.all_to_all(entering, "seq", split_axis=0, concat_axis=0, tiled=True)
    back, mark = near_call(1, gate, *near, mark)

    common = (x, cot, ahead, back, inverse, norm_gain, taps, fixed["spread"], enter)
    layer, grad, edge = finish_call(rows, 0, SPLIT, *common)
    on_low = shifted(layer, "section", 1)
    back_low = shifted(grad, "section", -1)
    layer, grad = finish_call(rows, SPLIT, rows - SPLIT, *common, edge)
    on_high = shifted(layer, "section", 1)
    back_high = shifted(grad, "section", -1)
    joined = join_call(rows, 0, on_low, back_low)
    passed_on, passed_back = join_call(rows, SPLIT, on_high, back_high, *joined)
    return passed_on[None], passed_back[None]


def solution(mesh):
    in_specs = (
        P("section", "seq", None),
        P("section", "seq", None),
        P("section", None),
        P("section", None, None, None),
        P("section", None, None),
        P("section", None, None),
        P("section", None),
    )
    out_specs = (P("section", "seq", None), P("section", "seq", None))
    return jax.shard_map(local, mesh=mesh, in_specs=in_specs, out_specs=out_specs, check_vma=False)
```

```python
import functools

import jax
import jax.numpy as jnp
import ml_dtypes
import numpy as np
from jax import lax
from jax.experimental import pallas as pl
from jax.experimental.pallas import tpu as pltpu
from jax.sharding import PartitionSpec as P

MODES = 16
NODES = 14
PADDED = 16
PACKET = 40
EXTRA = 32
LANES = 128
START_GROUP = 128
START_TOGETHER = 8
PROJECT_UNROLL = 8
PIECES = 4
SPLIT = 64
NEAR_STEP = 1024
NEAR_GROUP = 1024
FINISH_GROUP = 128
FINISH_TOGETHER = 8
F32 = jnp.float32
BF16 = jnp.bfloat16
shape = jax.ShapeDtypeStruct


def node_places(rows):
    k = np.arange(NODES)
    return 0.5 * (rows - 1) * (1.0 - np.cos((2 * k + 1) * np.pi / (2 * NODES)))


def cardinals(rows):
    nodes = node_places(rows)
    lags = np.arange(rows, dtype=np.float64)
    table = np.ones((rows, NODES))
    for k in range(NODES):
        for m in range(NODES):
            if m != k:
                table[:, k] *= (lags - nodes[m]) / (nodes[k] - nodes[m])
    return table


def halves(table):
    high = table.astype(ml_dtypes.bfloat16)
    low = (table - high.astype(np.float64)).astype(ml_dtypes.bfloat16)
    return high, low


def constants(rows):
    table = cardinals(rows)
    padded = np.zeros((rows, PADDED))
    padded[:, :NODES] = table
    high, low = halves(padded)
    flip_high, flip_low = high[::-1], low[::-1]
    moment_ahead = np.concatenate([flip_high.T, flip_low.T], axis=0)
    moment_back = np.concatenate([high.T, low.T], axis=0)
    first_rows = np.zeros((rows, PADDED), high.dtype)
    first_rows[0, NODES] = first_rows[1, NODES + 1] = 1.0
    spread_ahead = np.concatenate([high + first_rows, low], axis=1)
    spread_back = np.concatenate([flip_high + first_rows, flip_low], axis=1)
    lag = np.arange(rows)[:, None] - np.arange(rows)[None, :]
    toeplitz = np.where(lag[:, :, None] >= 0, table[np.maximum(lag, 0)], 0.0)
    near_ahead = np.transpose(toeplitz, (0, 2, 1)).reshape(rows, NODES * rows)
    near_back = np.transpose(toeplitz, (1, 2, 0)).reshape(rows, NODES * rows)
    places = np.zeros((PADDED, LANES), np.float32)
    places[:NODES] = node_places(rows)[:, None]
    cast = ml_dtypes.bfloat16
    return dict(
        moments=np.concatenate(
            [
                np.concatenate([moment_ahead, np.zeros_like(moment_ahead)], axis=1),
                np.concatenate([np.zeros_like(moment_back), moment_back], axis=1),
            ],
            axis=0,
        ),
        spread=np.concatenate([spread_ahead, spread_back], axis=0),
        near=np.stack([near_ahead, near_back]).astype(cast),
        places=places,
    )


def coefs_of(rates, residue):
    return residue * jnp.sqrt(1.0 - jnp.exp(-2.0 * rates))


def nodal_sum(rates, weight, places):
    places = wide(places, rates.shape[1])
    total = jnp.exp(-rates[0:1] * places) * weight[0:1]
    for r in range(1, MODES):
        total = total + jnp.exp(-rates[r : r + 1] * places) * weight[r : r + 1]
    return total


def taps_of(taps_ref, gain_ref, cols):
    gain = gain_ref[:, cols]
    return [[taps_ref[j, i, :, cols] * gain for i in range(3)] for j in range(3)]


def group_of(index, size=LANES):
    return pl.ds(pl.multiple_of(index * size, size), size)


def wide(block, width):
    return jnp.concatenate([block] * (width // LANES), axis=1)


def row_scale(block_sum, width):
    return lax.rsqrt(jnp.sum(block_sum, axis=1, keepdims=True) * (1.0 / width) + 1e-06)


def lane_sums(block):
    total = block[:, :LANES]
    for i in range(1, block.shape[1] // LANES):
        total = total + block[:, i * LANES : (i + 1) * LANES]
    return total


def filtered(taps, now, past, older):
    return [t[0] * now + t[1] * past + t[2] * older for t in taps]


def start_kernel(
    nodes, x_hbm, cot_hbm, gain_hbm, taps_hbm, rates_hbm, moments_hbm,
    mixed_hbm, gate_hbm, packet_hbm, inverse_hbm,
    x_ref, cot_ref, gain_ref, taps_ref, rates_ref, moments_ref, mixed_ref, gate_ref, packet_ref, inverse_ref,
    normed_refs, moment_ref, x_sems, cot_sems, table_sems, mixed_sems, gate_sems, last_sems,
):
    rows, width = x_ref.shape
    size = normed_refs.shape[2]
    pieces = x_sems.shape[0]
    part = width // pieces

    def piece(p):
        return slice(None), pl.ds(p * part, part)

    x_copies = [pltpu.make_async_copy(x_hbm.at[piece(p)], x_ref.at[piece(p)], x_sems.at[p]) for p in range(pieces)]
    cot_copies = [
        pltpu.make_async_copy(cot_hbm.at[piece(p)], cot_ref.at[piece(p)], cot_sems.at[p]) for p in range(pieces)
    ]
    table_copies = [
        pltpu.make_async_copy(source, target, table_sems.at[n])
        for n, (source, target) in enumerate(
            ((gain_hbm, gain_ref), (taps_hbm, taps_ref), (moments_hbm, moments_ref), (rates_hbm, rates_ref))
        )
    ]
    for copy in x_copies + table_copies + cot_copies:
        copy.start()

    for n in range(normed_refs.shape[0]):
        normed_refs[n, 0:8] = jnp.zeros((8, size), F32)
    total = jnp.zeros((rows, LANES), F32)
    for p in range(pieces):
        x_copies[p].wait()

        def square(i, total):
            x = x_ref[:, group_of(p * (part // LANES) + i)].astype(F32)
            return total + x * x

        total = lax.fori_loop(0, part // LANES, square, total, unroll=4)
    inverse_ref[...] = jnp.broadcast_to(row_scale(total, width), (rows, LANES))
    for copy in table_copies:
        copy.wait()

    lane = lax.broadcasted_iota(jnp.int32, (1, LANES), 1)
    scale = jnp.zeros((1, LANES), F32)
    for n, row in enumerate((0, 1, rows - 2, rows - 1)):
        scale = jnp.where(lane == n, inverse_ref[row : row + 1], scale)
    scale_high = scale.astype(BF16).astype(F32)
    scales = jnp.concatenate([scale_high, scale - scale_high], axis=0)

    def group(i, normed_ref):
        cols = group_of(i, size)
        now = x_ref[:, cols].astype(F32) * wide(inverse_ref[...], size)
        normed_ref[8 : rows + 8] = now
        past = normed_ref[7 : rows + 7]
        older = normed_ref[6 : rows + 6]
        query, key, value = filtered(taps_of(taps_ref, gain_ref, cols), now, past, older)
        kept = lax.broadcasted_iota(jnp.int32, (16, size), 0) >= 2
        for signal, out_ref in ((key * value, mixed_ref), (cot_ref[:, cols].astype(F32) * query, gate_ref)):
            head = jnp.where(kept, signal[0:16], 0.0)
            out_ref[:, cols] = jnp.concatenate([head, signal[16:]], axis=0).astype(BF16)

    together = normed_refs.shape[0]

    def groups(i, carry):
        for n in range(together):
            group(i * together + n, normed_refs.at[n])
        return carry

    def gather(p):
        cols = pl.ds(p * part, part)
        signals = jnp.concatenate([mixed_ref[:, cols], gate_ref[:, cols]], axis=0)
        both = jnp.dot(moments_ref[...], signals, preferred_element_type=F32)
        for side in range(2):
            high = 2 * PADDED * side
            moment_ref[PADDED * side : PADDED * (side + 1), cols] = (
                both[high : high + PADDED] + both[high + PADDED : high + 2 * PADDED]
            )

    def project(i, carry):
        cols = group_of(i)
        rates = rates_ref[:, cols]
        states = [0.0, 0.0]
        for k in range(NODES):
            power = jnp.exp(rates * (-nodes[k]))
            states = [
                states[side] + power * moment_ref[PADDED * side + k : PADDED * side + k + 1, cols]
                for side in range(2)
            ]
        x_head = x_ref[0:16, cols].astype(F32)
        x_tail = x_ref[rows - 16 : rows, cols].astype(F32)
        cot_head = cot_ref[0:16, cols].astype(F32)
        packet_ref[i] = jnp.concatenate(
            states + [x_head[0:2], x_tail[14:16], cot_head[0:2], scales], axis=0
        ).astype(BF16)
        return carry

    out_copies = []
    for p in range(pieces):
        cot_copies[p].wait()
        steps = part // size // together
        lax.fori_loop(p * steps, (p + 1) * steps, groups, 0)
        out_copies += [
            pltpu.make_async_copy(mixed_ref.at[piece(p)], mixed_hbm.at[piece(p)], mixed_sems.at[p]),
            pltpu.make_async_copy(gate_ref.at[piece(p)], gate_hbm.at[piece(p)], gate_sems.at[p]),
        ]
        for copy in out_copies[-2:]:
            copy.start()
        gather(p)
        lax.fori_loop(p * (part // LANES), (p + 1) * (part // LANES), project, 0, unroll=PROJECT_UNROLL)
    out_copies += [
        pltpu.make_async_copy(source, target, last_sems.at[n])
        for n, (source, target) in enumerate(
            ((packet_ref, packet_hbm), (inverse_ref, inverse_hbm))
        )
    ]
    for copy in out_copies[-2:]:
        copy.start()
    for copy in out_copies:
        copy.wait()


def near_kernel(
    signal_ref, rates_ref, residue_ref, places_ref, skip_ref, near_ref, mark_ref, out_ref, done_ref, parts_ref
):
    rows = signal_ref.shape[0]
    done_ref[...] = jnp.zeros_like(done_ref)
    size = min(NEAR_GROUP, signal_ref.shape[1])

    def group(i, carry):
        cols = group_of(i, size)
        rates = rates_ref[:, cols]
        nodal = nodal_sum(rates, coefs_of(rates, residue_ref[:, cols]), places_ref[...])
        signal = signal_ref[:, cols].astype(F32)
        for k in range(NODES):
            parts_ref[k * rows : (k + 1) * rows] = (signal * nodal[k : k + 1]).astype(BF16)
        out_ref[:, cols] = (
            jnp.dot(near_ref[0], parts_ref[...], preferred_element_type=F32)
            + skip_ref[:, cols] * signal
        )
        return carry

    lax.fori_loop(0, signal_ref.shape[1] // size, group, 0)


def over(block):
    return jnp.sum(block, axis=0, keepdims=True)


def scan_kernel(
    rates_ref, residue_ref, skip_ref, gain_ref, taps_ref, places_ref, packet_ref, mark_ref, enter_ref, done_ref,
    wide_ref, row_ref, base_ref, column_ref, *, rows,
):
    done_ref[...] = jnp.zeros_like(done_ref)
    count = packet_ref.shape[0]
    cols = pl.ds(pl.multiple_of(lax.axis_index("seq") * LANES, LANES), LANES)
    rates = rates_ref[:, cols]
    skip = skip_ref[:, cols]
    taps = taps_of(taps_ref, gain_ref, cols)
    coef = coefs_of(rates, residue_ref[:, cols])
    fall = jnp.exp(-rates)
    rise = jnp.exp(rates)
    now, later, earlier = over(coef), over(coef * fall), over(coef * rise)
    places = places_ref[...]
    for r in range(MODES):
        column_ref[r] = jnp.exp(-rates[r : r + 1] * places)
    for d in range(count):
        wide_ref[d * PACKET : (d + 1) * PACKET] = packet_ref[d].astype(F32)
    x_0, x_1, x_2, x_3, cot_0, cot_1, high, low = [
        wide_ref[pl.ds(EXTRA + n, count, stride=PACKET), :] for n in range(8)
    ]
    scale = high + low
    n_0, n_1, n_2, n_3 = [
        x * jnp.broadcast_to(scale[:, n : n + 1], (count, LANES)) for n, x in enumerate((x_0, x_1, x_2, x_3))
    ]
    zero = jnp.zeros((1, LANES), F32)

    def before(block):
        return jnp.concatenate([zero, block[:-1]], axis=0)

    def after(block):
        return jnp.concatenate([block[1:], zero], axis=0)

    n_2, n_3 = before(n_2), before(n_3)
    query_0, key_0, value_0 = filtered(taps, n_0, n_3, n_2)
    query_1, key_1, value_1 = filtered(taps, n_1, n_0, n_3)
    mixed_0, mixed_1, gate_0, gate_1 = [
        block.astype(BF16).astype(F32)
        for block in (key_0 * value_0, key_1 * value_1, cot_0 * query_0, cot_1 * query_1)
    ]
    rows_kept = (
        mixed_0,
        mixed_1,
        gate_0,
        gate_1,
        skip * mixed_0 - earlier * mixed_1,
        skip * mixed_1,
        (now + skip) * gate_0 + later * gate_1,
        (now + skip) * gate_1,
    )
    for n, block in enumerate(rows_kept):
        row_ref[n] = block

    decay = jnp.exp(rates * (-float(rows)))
    lead_0 = jnp.exp(rates * (1.0 - rows))
    lead_1 = jnp.exp(rates * (2.0 - rows))

    def spread(weight):
        total = column_ref[0] * weight[0:1]
        for r in range(1, MODES):
            total = total + column_ref[r] * weight[r : r + 1]
        return total[0:NODES]

    ahead = jnp.zeros((MODES, LANES), F32)
    back = jnp.zeros((MODES, LANES), F32)
    for step in range(count):
        d = step
        reached = coef * fall * ahead
        base_ref[0, d : d + 1] = over(reached)
        base_ref[1, d : d + 1] = over(reached * fall)
        nodal = spread(reached + coef * (row_ref[0, d : d + 1] + rise * row_ref[1, d : d + 1]))
        own = wide_ref[d * PACKET : d * PACKET + MODES]
        wide_ref[d * PACKET : d * PACKET + PADDED] = jnp.concatenate(
            [nodal, row_ref[4, d : d + 1], row_ref[5, d : d + 1]], axis=0
        )
        ahead = decay * ahead + (own + lead_0 * row_ref[0, d : d + 1] + lead_1 * row_ref[1, d : d + 1])

        d = count - 1 - step
        nodal = spread(coef * fall * back)
        back = decay * back + wide_ref[d * PACKET + MODES : d * PACKET + 2 * MODES]
        wide_ref[d * PACKET + PADDED : d * PACKET + 2 * PADDED] = jnp.concatenate(
            [nodal, row_ref[6, d : d + 1], row_ref[7, d : d + 1]], axis=0
        )
        reached = coef * back
        base_ref[2, d : d + 1] = over(reached)
        base_ref[3, d : d + 1] = over(reached * rise)
        back = back + row_ref[2, d : d + 1] + fall * row_ref[3, d : d + 1]

    conv_0 = base_ref[0] + (now + skip) * mixed_0
    conv_1 = base_ref[1] + later * mixed_0 + (now + skip) * mixed_1
    back_0 = base_ref[2] + row_ref[6]
    back_1 = base_ref[3] + row_ref[7]
    conv_0, conv_1, back_0, back_1 = [block.astype(BF16).astype(F32) for block in (conv_0, conv_1, back_0, back_1)]
    grads_0 = (cot_0 * conv_0, back_0 * value_0, back_0 * key_0)
    grads_1 = (cot_1 * conv_1, back_1 * value_1, back_1 * key_1)
    edges = (
        before(x_2),
        before(x_3),
        after(sum(taps[j][1] * grads_0[j] for j in range(3))),
        after(sum(taps[j][2] * grads_0[j] for j in range(3))),
        after(sum(taps[j][2] * grads_1[j] for j in range(3))),
    )
    for n, block in enumerate(edges):
        row_ref[n] = block
    unused = jnp.zeros((PACKET - EXTRA - len(edges), LANES), F32)
    for d in range(count):
        extra = [row_ref[n, d : d + 1] for n in range(len(edges))]
        wide_ref[d * PACKET + EXTRA : (d + 1) * PACKET] = jnp.concatenate(extra + [unused], axis=0)
        enter_ref[d] = wide_ref[d * PACKET : (d + 1) * PACKET].astype(BF16)


def finish_kernel(
    rows, first, count, x_hbm, cot_hbm, ahead_hbm, back_hbm, inverse_ref, gain_ref, taps_ref, spread_ref, enter_ref,
    *refs,
):
    low = first == 0
    if low:
        grad_ref, layer_ref, edge_ref, *refs = refs
    else:
        edge_ref, grad_ref, layer_ref, *refs = refs
    (
        x_ref, cot_ref, ahead_ref, back_ref, base_ref, normed_refs, one_refs, two_refs, total_ref, load_sems,
    ) = refs
    width = x_ref.shape[1]
    size = normed_refs.shape[2]
    together = normed_refs.shape[0]
    pieces = load_sems.shape[1]
    part = width // pieces
    top = 0 if low else 16
    reach = count + 8 if low else count

    def lanes(p):
        return pl.ds(p * part, part)

    loads = []
    for p in range(pieces):
        loads.append([
            pltpu.make_async_copy(
                source.at[pl.ds(lo, target.shape[0]), lanes(p)], target.at[:, lanes(p)], load_sems.at[k, p]
            )
            for k, (source, target, lo) in enumerate((
                (x_hbm, x_ref, first - top),
                (cot_hbm, cot_ref, first),
                (ahead_hbm, ahead_ref, first),
                (back_hbm, back_ref, first),
            ))
        ])
        for copy in loads[p]:
            copy.start()

    total_ref[...] = jnp.zeros_like(total_ref)
    if low:
        def edges(j, total):
            block = enter_ref[j].astype(F32)[EXTRA:PACKET]
            edge_ref[0:8, group_of(j)] = block
            return total + block * block

        total = lax.fori_loop(0, width // LANES, edges, jnp.zeros((8, LANES), F32), unroll=4)
        edge_ref[8:16, 0:LANES] = jnp.broadcast_to(row_scale(total, width), (8, LANES))

    edge_scale = wide(edge_ref[8:16, 0:LANES], size)
    inverse = wide(inverse_ref[first : first + reach], size)
    blocks = size // LANES

    def group(i, normed_ref, one_ref, two_ref):
        cols = group_of(i, size)
        taps = taps_of(taps_ref, gain_ref, cols)
        x = x_ref[top:, cols].astype(F32)[0:reach]
        cot = cot_ref[:, cols].astype(F32)[0:reach]
        normed_ref[16 : reach + 16] = x * inverse
        if low:
            normed_ref[14:16] = edge_ref[0:2, cols] * edge_scale[0:2]
        else:
            above = x_ref[0:16, cols].astype(F32)
            normed_ref[0:16] = above * wide(inverse_ref[first - 16 : first], size)
        now = normed_ref[16 : reach + 16]
        past = normed_ref[15 : reach + 15]
        older = normed_ref[14 : reach + 14]
        query, key, value = filtered(taps, now, past, older)

        convs = []
        for side, near_ref in enumerate((ahead_ref, back_ref)):
            nodal = jnp.concatenate(
                [enter_ref[i * blocks + h, PADDED * side : PADDED * (side + 1)] for h in range(blocks)], axis=1
            )
            far = jnp.dot(
                spread_ref[side * rows + first : side * rows + first + cot_ref.shape[0]],
                jnp.concatenate([nodal, nodal], axis=0),
                preferred_element_type=F32,
            )
            total = near_ref[:, cols] + far[0:reach]
            convs.append(total.astype(BF16).astype(F32))
        conv, conv_back = convs
        layer_ref[:, cols] = (x[0:count] + query[0:count] * conv[0:count]).astype(BF16)

        grads = (cot * conv, conv_back * value, conv_back * key)
        lagged = [sum(taps[j][i] * grads[j] for j in range(3)) for i in range(3)]
        one_ref[0:reach] = lagged[1]
        two_ref[0:reach] = lagged[2]
        if not low:
            one_ref[count : count + 1] = edge_ref[2:3, cols]
            two_ref[count : count + 2] = edge_ref[3:5, cols]
        scaled = lagged[0][0:count] + one_ref[1 : count + 1] + two_ref[2 : count + 2]
        base_ref[:, cols] = cot[0:count] + inverse[0:count] * scaled
        return lane_sums(scaled * x[0:count])

    def groups(i, carry):
        sums = [group(i * together + n, normed_refs.at[n], one_refs.at[n], two_refs.at[n]) for n in range(together)]
        total_ref[...] = total_ref[...] + sum(sums)
        return carry

    for p in range(pieces):
        for copy in loads[p]:
            copy.wait()
        steps = part // size // together
        lax.fori_loop(p * steps, (p + 1) * steps, groups, 0)

    mean = jnp.sum(total_ref[...], axis=1, keepdims=True) * (1.0 / width)
    scale = inverse_ref[first : first + count]
    factor = scale * scale * scale * jnp.broadcast_to(mean, (count, LANES))

    def emit(i, carry):
        cols = group_of(i)
        x = x_ref[top : top + count, cols].astype(F32)
        grad_ref[:, cols] = (base_ref[:, cols] - x * factor).astype(BF16)
        return carry

    lax.fori_loop(0, width // LANES, emit, 0, unroll=4)


def join_kernel(first, grad_ref, layer_ref, *refs):
    grad_hbm, layer_hbm, sems = refs[-3:]
    count = layer_ref.shape[0]
    half = layer_ref.shape[1] // 2
    copies = []
    for n, (source, target) in enumerate(((grad_ref, grad_hbm), (layer_ref, layer_hbm))):
        for h in range(2):
            lanes = pl.ds(h * half, half)
            copies.append(
                pltpu.make_async_copy(source.at[:, lanes], target.at[pl.ds(first, count), lanes], sems.at[n, h])
            )
    for copy in copies:
        copy.start()
    for copy in copies:
        copy.wait()


def shifted(block, axis, distance):
    devices = range(lax.axis_size(axis))
    route = [(i - distance, i) for i in devices if i - distance in devices]
    return lax.ppermute(block, axis, route)


def whole(shape):
    return pl.BlockSpec(shape, lambda *i: (0,) * len(shape))


def across(shape, step, axis=None):
    axis = len(shape) - 1 if axis is None else axis
    block = shape[:axis] + (step,) + shape[axis + 1 :]
    return pl.BlockSpec(block, lambda i: (0,) * axis + (i,) + (0,) * (len(shape) - axis - 1))


def params(mib):
    return pltpu.CompilerParams(vmem_limit_bytes=mib << 20)


def stay(array):
    return pltpu.with_memory_space_constraint(array, pltpu.HBM)


def takes(micros):
    return pl.CostEstimate(
        flops=int(micros * 1.1e9), bytes_accessed=int(micros * 3.5e6), transcendentals=0
    )


def start_call(x, cot, gain, taps, rates, moments):
    rows, width = x.shape
    pieces = PIECES
    far = pl.BlockSpec(memory_space=pltpu.HBM)
    outs = [
        (x.shape, BF16),
        (x.shape, BF16),
        ((width // LANES, PACKET, LANES), BF16),
        ((rows, LANES), F32),
    ]
    ins = (x, cot, gain, taps, rates, moments)
    held = (x, cot, gain, taps, rates, moments)
    return pl.pallas_call(
        functools.partial(start_kernel, [float(p) for p in node_places(rows)]),
        in_specs=[far] * len(ins),
        out_specs=[far] * len(outs),
        out_shape=[pltpu.HBM(*out) for out in outs],
        scratch_shapes=[pltpu.VMEM(array.shape, array.dtype) for array in held]
        + [pltpu.VMEM(*out) for out in outs]
        + [
            pltpu.VMEM((min(START_TOGETHER, width // pieces // START_GROUP), rows + 8, START_GROUP), F32),
            pltpu.VMEM((2 * PADDED, width), F32),
            pltpu.SemaphoreType.DMA((pieces,)),
            pltpu.SemaphoreType.DMA((pieces,)),
            pltpu.SemaphoreType.DMA((4,)),
            pltpu.SemaphoreType.DMA((pieces,)),
            pltpu.SemaphoreType.DMA((pieces,)),
            pltpu.SemaphoreType.DMA((2,)),
        ],
        compiler_params=params(24),
        cost_estimate=takes(6),
        name="start",
    )(*[stay(array) for array in ins])


def near_call(side, signal, rates, residue, places, skip, near, mark):
    rows, width = signal.shape
    step = min(NEAR_STEP, width)
    return pl.pallas_call(
        near_kernel,
        grid=(width // step,),
        in_specs=[
            across(signal.shape, step),
            across(rates.shape, step), across(rates.shape, step), whole(places.shape),
            across(skip.shape, step),
            pl.BlockSpec((1,) + near.shape[1:], lambda i: (side, 0, 0)),
            whole((8, LANES)),
        ],
        out_specs=[across(signal.shape, step), whole((8, LANES))],
        out_shape=[pltpu.HBM(signal.shape, F32), shape((8, LANES), F32)],
        scratch_shapes=[pltpu.VMEM((NODES * rows, min(NEAR_GROUP, width)), BF16)],
        compiler_params=params(16),
        cost_estimate=takes(4),
        name="near",
    )(stay(signal), rates, residue, places, skip, stay(near), mark)


def scan_call(rates, residue, skip, gain, taps, places, gathered, mark, rows):
    count = gathered.shape[0]
    return pl.pallas_call(
        functools.partial(scan_kernel, rows=rows),
        out_shape=[shape(gathered.shape, BF16), shape((8, LANES), F32)],
        scratch_shapes=[
            pltpu.VMEM((count * PACKET, LANES), F32),
            pltpu.VMEM((8, count, LANES), F32),
            pltpu.VMEM((4, count, LANES), F32),
            pltpu.VMEM((MODES, PADDED, LANES), F32),
        ],
        compiler_params=params(8),
        cost_estimate=takes(2),
        name="scan",
    )(rates, residue, skip, gain, taps, places, gathered, mark)


def finish_call(rows, first, count, *arrays):
    x = arrays[0]
    width = x.shape[1]
    low = first == 0
    pieces = PIECES
    size = min(FINISH_GROUP, width)
    together = min(FINISH_TOGETHER, width // pieces // size)
    far = pl.BlockSpec(memory_space=pltpu.HBM)
    near = pl.BlockSpec(memory_space=pltpu.VMEM)
    half = shape((count, width), BF16)
    out_shape = [half, half]
    above, below, reach = (0, 16, count + 8) if low else (16, 0, count)
    if low:
        out_shape += [shape((16, width), F32)]
    return pl.pallas_call(
        functools.partial(finish_kernel, rows, first, count),
        in_specs=[far] * 4 + [near] * (len(arrays) - 4),
        out_specs=[near] * len(out_shape),
        out_shape=out_shape,
        scratch_shapes=[
            pltpu.VMEM((above + count + below, width), BF16),
            pltpu.VMEM((count + below, width), BF16),
            pltpu.VMEM((reach, width), F32),
            pltpu.VMEM((reach, width), F32),
            pltpu.VMEM((count, width), F32),
            pltpu.VMEM((together, reach + 24, size), F32),
            pltpu.VMEM((together, reach + 8, size), F32),
            pltpu.VMEM((together, reach + 8, size), F32),
            pltpu.VMEM((count, LANES), F32),
            pltpu.SemaphoreType.DMA((4, pieces)),
        ],
        compiler_params=params(24),
        cost_estimate=takes(6),
        name="finish",
    )(*[stay(array) for array in arrays[:4]], *arrays[4:])


def join_call(rows, first, grad, layer, *wholes):
    far = pl.BlockSpec(memory_space=pltpu.HBM)
    near = pl.BlockSpec(memory_space=pltpu.VMEM)
    out = shape((rows, layer.shape[1]), BF16)
    return pl.pallas_call(
        functools.partial(join_kernel, first),
        in_specs=[near, near] + [far] * len(wholes),
        out_specs=[far, far],
        out_shape=[out, out],
        scratch_shapes=[pltpu.SemaphoreType.DMA((2, 2))],
        input_output_aliases={2 + n: n for n in range(len(wholes))},
        compiler_params=params(4),
        cost_estimate=takes(1),
        name="join",
    )(grad, layer, *wholes)


def local(section_input, cotangent, norm_gain, short_filter, decay_rate, residue, skip_gain):
    x = section_input[0]
    cot = cotangent[0]
    rows = x.shape[0]
    taps = jnp.transpose(short_filter, (1, 2, 0, 3))
    rates = decay_rate[0]
    fixed = {name: jnp.asarray(table) for name, table in constants(rows).items()}

    weights = residue[0]
    mixed, gate, packet, inverse = start_call(x, cot, norm_gain, taps, rates, fixed["moments"])
    gathered = lax.all_to_all(packet, "seq", split_axis=0, concat_axis=0, tiled=True)
    near = (rates, weights, fixed["places"], skip_gain, fixed["near"])
    ahead, mark = near_call(0, mixed, *near, stay(inverse))
    entering, mark = scan_call(rates, weights, skip_gain, norm_gain, taps, fixed["places"], gathered, mark, rows)
    enter = lax.all_to_all(entering, "seq", split_axis=0, concat_axis=0, tiled=True)
    back, mark = near_call(1, gate, *near, mark)

    common = (x, cot, ahead, back, inverse, norm_gain, taps, fixed["spread"], enter)
    grad, layer, edge = finish_call(rows, 0, SPLIT, *common)
    back_low = shifted(grad, "section", -1)
    on_low = shifted(layer, "section", 1)
    grad, layer = finish_call(rows, SPLIT, rows - SPLIT, *common, edge)
    back_high = shifted(grad, "section", -1)
    on_high = shifted(layer, "section", 1)
    joined = join_call(rows, 0, back_low, on_low)
    passed_back, passed_on = join_call(rows, SPLIT, back_high, on_high, *joined)
    return passed_on[None], passed_back[None]


def solution(mesh):
    in_specs = (
        P("section", "seq", None),
        P("section", "seq", None),
        P("section", None),
        P("section", None, None, None),
        P("section", None, None),
        P("section", None, None),
        P("section", None),
    )
    out_specs = (P("section", "seq", None), P("section", "seq", None))
    return jax.shard_map(local, mesh=mesh, in_specs=in_specs, out_specs=out_specs, check_vma=False)
```

```python
import functools

import jax
import jax.numpy as jnp
import ml_dtypes
import numpy as np
from jax import lax
from jax.experimental import pallas as pl
from jax.experimental.pallas import tpu as pltpu
from jax.sharding import PartitionSpec as P

MODES = 16
NODES = 14
PADDED = 16
PACKET = 40
EXTRA = 32
LANES = 128
START_GROUP = 128
START_TOGETHER = 8
PROJECT_UNROLL = 8
PIECES = 4
SPLIT = 64
NEAR_STEP = 1024
NEAR_GROUP = 1024
FINISH_GROUP = 128
FINISH_TOGETHER = 8
F32 = jnp.float32
BF16 = jnp.bfloat16
shape = jax.ShapeDtypeStruct


def node_places(rows):
    k = np.arange(NODES)
    return 0.5 * (rows - 1) * (1.0 - np.cos((2 * k + 1) * np.pi / (2 * NODES)))


def cardinals(rows):
    nodes = node_places(rows)
    lags = np.arange(rows, dtype=np.float64)
    table = np.ones((rows, NODES))
    for k in range(NODES):
        for m in range(NODES):
            if m != k:
                table[:, k] *= (lags - nodes[m]) / (nodes[k] - nodes[m])
    return table


def halves(table):
    high = table.astype(ml_dtypes.bfloat16)
    low = (table - high.astype(np.float64)).astype(ml_dtypes.bfloat16)
    return high, low


def constants(rows):
    table = cardinals(rows)
    padded = np.zeros((rows, PADDED))
    padded[:, :NODES] = table
    high, low = halves(padded)
    flip_high, flip_low = high[::-1], low[::-1]
    moment_ahead = np.concatenate([flip_high.T, flip_low.T], axis=0)
    moment_back = np.concatenate([high.T, low.T], axis=0)
    first_rows = np.zeros((rows, PADDED), high.dtype)
    first_rows[0, NODES] = first_rows[1, NODES + 1] = 1.0
    spread_ahead = np.concatenate([high + first_rows, low], axis=1)
    spread_back = np.concatenate([flip_high + first_rows, flip_low], axis=1)
    lag = np.arange(rows)[:, None] - np.arange(rows)[None, :]
    toeplitz = np.where(lag[:, :, None] >= 0, table[np.maximum(lag, 0)], 0.0)
    near_ahead = np.transpose(toeplitz, (0, 2, 1)).reshape(rows, NODES * rows)
    near_back = np.transpose(toeplitz, (1, 2, 0)).reshape(rows, NODES * rows)
    places = np.zeros((PADDED, LANES), np.float32)
    places[:NODES] = node_places(rows)[:, None]
    cast = ml_dtypes.bfloat16
    return dict(
        moments=np.concatenate(
            [
                np.concatenate([moment_ahead, np.zeros_like(moment_ahead)], axis=1),
                np.concatenate([np.zeros_like(moment_back), moment_back], axis=1),
            ],
            axis=0,
        ),
        spread=np.concatenate([spread_ahead, spread_back], axis=0),
        near=np.stack([near_ahead, near_back]).astype(cast),
        places=places,
    )


def coefs_of(rates, residue):
    return residue * jnp.sqrt(1.0 - jnp.exp(-2.0 * rates))


def nodal_sum(rates, weight, places):
    places = wide(places, rates.shape[1])
    total = jnp.exp(-rates[0:1] * places) * weight[0:1]
    for r in range(1, MODES):
        total = total + jnp.exp(-rates[r : r + 1] * places) * weight[r : r + 1]
    return total


def taps_of(taps_ref, gain_ref, cols):
    gain = gain_ref[:, cols]
    return [[taps_ref[j, i, :, cols] * gain for i in range(3)] for j in range(3)]


def group_of(index, size=LANES):
    return pl.ds(pl.multiple_of(index * size, size), size)


def wide(block, width):
    return jnp.concatenate([block] * (width // LANES), axis=1)


def row_scale(block_sum, width):
    return lax.rsqrt(jnp.sum(block_sum, axis=1, keepdims=True) * (1.0 / width) + 1e-06)


def lane_sums(block):
    total = block[:, :LANES]
    for i in range(1, block.shape[1] // LANES):
        total = total + block[:, i * LANES : (i + 1) * LANES]
    return total


def filtered(taps, now, past, older):
    return [t[0] * now + t[1] * past + t[2] * older for t in taps]


def start_kernel(
    x_hbm, cot_hbm, gain_hbm, taps_hbm, moments_hbm,
    mixed_hbm, gate_hbm, packet_hbm, inverse_hbm,
    x_ref, cot_ref, gain_ref, taps_ref, moments_ref, mixed_ref, gate_ref, packet_ref, inverse_ref,
    normed_refs, moment_ref, x_sems, cot_sems, table_sems, mixed_sems, gate_sems, last_sems,
):
    rows, width = x_ref.shape
    size = normed_refs.shape[2]
    pieces = x_sems.shape[0]
    part = width // pieces

    def piece(p):
        return slice(None), pl.ds(p * part, part)

    x_copies = [pltpu.make_async_copy(x_hbm.at[piece(p)], x_ref.at[piece(p)], x_sems.at[p]) for p in range(pieces)]
    cot_copies = [
        pltpu.make_async_copy(cot_hbm.at[piece(p)], cot_ref.at[piece(p)], cot_sems.at[p]) for p in range(pieces)
    ]
    table_copies = [
        pltpu.make_async_copy(source, target, table_sems.at[n])
        for n, (source, target) in enumerate(
            ((gain_hbm, gain_ref), (taps_hbm, taps_ref), (moments_hbm, moments_ref))
        )
    ]
    for copy in x_copies + table_copies + cot_copies:
        copy.start()

    for n in range(normed_refs.shape[0]):
        normed_refs[n, 0:8] = jnp.zeros((8, size), F32)
    total = jnp.zeros((rows, LANES), F32)
    for p in range(pieces):
        x_copies[p].wait()

        def square(i, total):
            x = x_ref[:, group_of(p * (part // LANES) + i)].astype(F32)
            return total + x * x

        total = lax.fori_loop(0, part // LANES, square, total, unroll=4)
    inverse_ref[...] = jnp.broadcast_to(row_scale(total, width), (rows, LANES))
    for copy in table_copies:
        copy.wait()

    lane = lax.broadcasted_iota(jnp.int32, (1, LANES), 1)
    scale = jnp.zeros((1, LANES), F32)
    for n, row in enumerate((0, 1, rows - 2, rows - 1)):
        scale = jnp.where(lane == n, inverse_ref[row : row + 1], scale)
    scale_high = scale.astype(BF16).astype(F32)
    scales = jnp.concatenate([scale_high, scale - scale_high], axis=0)

    def group(i, normed_ref):
        cols = group_of(i, size)
        now = x_ref[:, cols].astype(F32) * wide(inverse_ref[...], size)
        normed_ref[8 : rows + 8] = now
        past = normed_ref[7 : rows + 7]
        older = normed_ref[6 : rows + 6]
        query, key, value = filtered(taps_of(taps_ref, gain_ref, cols), now, past, older)
        kept = lax.broadcasted_iota(jnp.int32, (16, size), 0) >= 2
        for signal, out_ref in ((key * value, mixed_ref), (cot_ref[:, cols].astype(F32) * query, gate_ref)):
            head = jnp.where(kept, signal[0:16], 0.0)
            out_ref[:, cols] = jnp.concatenate([head, signal[16:]], axis=0).astype(BF16)

    together = normed_refs.shape[0]

    def groups(i, carry):
        for n in range(together):
            group(i * together + n, normed_refs.at[n])
        return carry

    def gather(p):
        cols = pl.ds(p * part, part)
        signals = jnp.concatenate([mixed_ref[:, cols], gate_ref[:, cols]], axis=0)
        both = jnp.dot(moments_ref[...], signals, preferred_element_type=F32)
        for side in range(2):
            high = 2 * PADDED * side
            moment_ref[PADDED * side : PADDED * (side + 1), cols] = (
                both[high : high + PADDED] + both[high + PADDED : high + 2 * PADDED]
            )

    def project(i, carry):
        cols = group_of(i)
        x_head = x_ref[0:16, cols].astype(F32)
        x_tail = x_ref[rows - 16 : rows, cols].astype(F32)
        cot_head = cot_ref[0:16, cols].astype(F32)
        packet_ref[i] = jnp.concatenate(
            [moment_ref[:, cols], x_head[0:2], x_tail[14:16], cot_head[0:2], scales], axis=0
        ).astype(BF16)
        return carry

    out_copies = []
    for p in range(pieces):
        cot_copies[p].wait()
        steps = part // size // together
        lax.fori_loop(p * steps, (p + 1) * steps, groups, 0)
        out_copies += [
            pltpu.make_async_copy(mixed_ref.at[piece(p)], mixed_hbm.at[piece(p)], mixed_sems.at[p]),
            pltpu.make_async_copy(gate_ref.at[piece(p)], gate_hbm.at[piece(p)], gate_sems.at[p]),
        ]
        for copy in out_copies[-2:]:
            copy.start()
        gather(p)
        lax.fori_loop(p * (part // LANES), (p + 1) * (part // LANES), project, 0, unroll=PROJECT_UNROLL)
    out_copies += [
        pltpu.make_async_copy(source, target, last_sems.at[n])
        for n, (source, target) in enumerate(
            ((packet_ref, packet_hbm), (inverse_ref, inverse_hbm))
        )
    ]
    for copy in out_copies[-2:]:
        copy.start()
    for copy in out_copies:
        copy.wait()


def near_kernel(
    signal_ref, rates_ref, residue_ref, places_ref, skip_ref, near_ref, mark_ref, out_ref, done_ref, parts_ref
):
    rows = signal_ref.shape[0]
    done_ref[...] = jnp.zeros_like(done_ref)
    size = min(NEAR_GROUP, signal_ref.shape[1])

    def group(i, carry):
        cols = group_of(i, size)
        rates = rates_ref[:, cols]
        nodal = nodal_sum(rates, coefs_of(rates, residue_ref[:, cols]), places_ref[...])
        signal = signal_ref[:, cols].astype(F32)
        for k in range(NODES):
            parts_ref[k * rows : (k + 1) * rows] = (signal * nodal[k : k + 1]).astype(BF16)
        out_ref[:, cols] = (
            jnp.dot(near_ref[0], parts_ref[...], preferred_element_type=F32)
            + skip_ref[:, cols] * signal
        )
        return carry

    lax.fori_loop(0, signal_ref.shape[1] // size, group, 0)


def over(block):
    return jnp.sum(block, axis=0, keepdims=True)


def scan_kernel(
    rates_ref, residue_ref, skip_ref, gain_ref, taps_ref, places_ref, packet_ref, mark_ref, enter_ref, done_ref,
    wide_ref, row_ref, base_ref, column_ref, power_ref, *, rows, nodes,
):
    done_ref[...] = jnp.zeros_like(done_ref)
    count = packet_ref.shape[0]
    cols = pl.ds(pl.multiple_of(lax.axis_index("seq") * LANES, LANES), LANES)
    rates = rates_ref[:, cols]
    skip = skip_ref[:, cols]
    taps = taps_of(taps_ref, gain_ref, cols)
    coef = coefs_of(rates, residue_ref[:, cols])
    fall = jnp.exp(-rates)
    rise = jnp.exp(rates)
    now, later, earlier = over(coef), over(coef * fall), over(coef * rise)
    places = places_ref[...]
    for r in range(MODES):
        column_ref[r] = jnp.exp(-rates[r : r + 1] * places)
    for k in range(NODES):
        power_ref[k] = jnp.exp(rates * (-nodes[k]))
    for d in range(count):
        wide_ref[d * PACKET : (d + 1) * PACKET] = packet_ref[d].astype(F32)
    x_0, x_1, x_2, x_3, cot_0, cot_1, high, low = [
        wide_ref[pl.ds(EXTRA + n, count, stride=PACKET), :] for n in range(8)
    ]
    scale = high + low
    n_0, n_1, n_2, n_3 = [
        x * jnp.broadcast_to(scale[:, n : n + 1], (count, LANES)) for n, x in enumerate((x_0, x_1, x_2, x_3))
    ]
    zero = jnp.zeros((1, LANES), F32)

    def before(block):
        return jnp.concatenate([zero, block[:-1]], axis=0)

    def after(block):
        return jnp.concatenate([block[1:], zero], axis=0)

    n_2, n_3 = before(n_2), before(n_3)
    query_0, key_0, value_0 = filtered(taps, n_0, n_3, n_2)
    query_1, key_1, value_1 = filtered(taps, n_1, n_0, n_3)
    mixed_0, mixed_1, gate_0, gate_1 = [
        block.astype(BF16).astype(F32)
        for block in (key_0 * value_0, key_1 * value_1, cot_0 * query_0, cot_1 * query_1)
    ]
    rows_kept = (
        mixed_0,
        mixed_1,
        gate_0,
        gate_1,
        skip * mixed_0 - earlier * mixed_1,
        skip * mixed_1,
        (now + skip) * gate_0 + later * gate_1,
        (now + skip) * gate_1,
    )
    for n, block in enumerate(rows_kept):
        row_ref[n] = block

    decay = jnp.exp(rates * (-float(rows)))
    lead_0 = jnp.exp(rates * (1.0 - rows))
    lead_1 = jnp.exp(rates * (2.0 - rows))

    def spread(weight):
        total = column_ref[0] * weight[0:1]
        for r in range(1, MODES):
            total = total + column_ref[r] * weight[r : r + 1]
        return total[0:NODES]

    def project(row):
        total = power_ref[0] * wide_ref[row : row + 1]
        for k in range(1, NODES):
            total = total + power_ref[k] * wide_ref[row + k : row + k + 1]
        return total

    ahead = jnp.zeros((MODES, LANES), F32)
    back = jnp.zeros((MODES, LANES), F32)
    for step in range(count):
        d = step
        reached = coef * fall * ahead
        base_ref[0, d : d + 1] = over(reached)
        base_ref[1, d : d + 1] = over(reached * fall)
        nodal = spread(reached + coef * (row_ref[0, d : d + 1] + rise * row_ref[1, d : d + 1]))
        own = project(d * PACKET)
        wide_ref[d * PACKET : d * PACKET + PADDED] = jnp.concatenate(
            [nodal, row_ref[4, d : d + 1], row_ref[5, d : d + 1]], axis=0
        )
        ahead = decay * ahead + (own + lead_0 * row_ref[0, d : d + 1] + lead_1 * row_ref[1, d : d + 1])

        d = count - 1 - step
        nodal = spread(coef * fall * back)
        back = decay * back + project(d * PACKET + PADDED)
        wide_ref[d * PACKET + PADDED : d * PACKET + 2 * PADDED] = jnp.concatenate(
            [nodal, row_ref[6, d : d + 1], row_ref[7, d : d + 1]], axis=0
        )
        reached = coef * back
        base_ref[2, d : d + 1] = over(reached)
        base_ref[3, d : d + 1] = over(reached * rise)
        back = back + row_ref[2, d : d + 1] + fall * row_ref[3, d : d + 1]

    conv_0 = base_ref[0] + (now + skip) * mixed_0
    conv_1 = base_ref[1] + later * mixed_0 + (now + skip) * mixed_1
    back_0 = base_ref[2] + row_ref[6]
    back_1 = base_ref[3] + row_ref[7]
    conv_0, conv_1, back_0, back_1 = [block.astype(BF16).astype(F32) for block in (conv_0, conv_1, back_0, back_1)]
    grads_0 = (cot_0 * conv_0, back_0 * value_0, back_0 * key_0)
    grads_1 = (cot_1 * conv_1, back_1 * value_1, back_1 * key_1)
    edges = (
        before(x_2),
        before(x_3),
        after(sum(taps[j][1] * grads_0[j] for j in range(3))),
        after(sum(taps[j][2] * grads_0[j] for j in range(3))),
        after(sum(taps[j][2] * grads_1[j] for j in range(3))),
    )
    for n, block in enumerate(edges):
        row_ref[n] = block
    unused = jnp.zeros((PACKET - EXTRA - len(edges), LANES), F32)
    for d in range(count):
        extra = [row_ref[n, d : d + 1] for n in range(len(edges))]
        wide_ref[d * PACKET + EXTRA : (d + 1) * PACKET] = jnp.concatenate(extra + [unused], axis=0)
        enter_ref[d] = wide_ref[d * PACKET : (d + 1) * PACKET].astype(BF16)


def finish_kernel(
    rows, first, count, x_hbm, cot_hbm, ahead_hbm, back_hbm, inverse_ref, gain_ref, taps_ref, spread_ref, enter_ref,
    *refs,
):
    low = first == 0
    if low:
        grad_ref, layer_ref, edge_ref, *refs = refs
    else:
        edge_ref, grad_ref, layer_ref, *refs = refs
    (
        x_ref, cot_ref, ahead_ref, back_ref, base_ref, normed_refs, one_refs, two_refs, total_ref, load_sems,
    ) = refs
    width = x_ref.shape[1]
    size = normed_refs.shape[2]
    together = normed_refs.shape[0]
    pieces = load_sems.shape[1]
    part = width // pieces
    top = 0 if low else 16
    reach = count + 8 if low else count

    def lanes(p):
        return pl.ds(p * part, part)

    loads = []
    for p in range(pieces):
        loads.append([
            pltpu.make_async_copy(
                source.at[pl.ds(lo, target.shape[0]), lanes(p)], target.at[:, lanes(p)], load_sems.at[k, p]
            )
            for k, (source, target, lo) in enumerate((
                (x_hbm, x_ref, first - top),
                (cot_hbm, cot_ref, first),
                (ahead_hbm, ahead_ref, first),
                (back_hbm, back_ref, first),
            ))
        ])
        for copy in loads[p]:
            copy.start()

    total_ref[...] = jnp.zeros_like(total_ref)
    if low:
        def edges(j, total):
            block = enter_ref[j].astype(F32)[EXTRA:PACKET]
            edge_ref[0:8, group_of(j)] = block
            return total + block * block

        total = lax.fori_loop(0, width // LANES, edges, jnp.zeros((8, LANES), F32), unroll=4)
        edge_ref[8:16, 0:LANES] = jnp.broadcast_to(row_scale(total, width), (8, LANES))

    edge_scale = wide(edge_ref[8:16, 0:LANES], size)
    inverse = wide(inverse_ref[first : first + reach], size)
    blocks = size // LANES

    def group(i, normed_ref, one_ref, two_ref):
        cols = group_of(i, size)
        taps = taps_of(taps_ref, gain_ref, cols)
        x = x_ref[top:, cols].astype(F32)[0:reach]
        cot = cot_ref[:, cols].astype(F32)[0:reach]
        normed_ref[16 : reach + 16] = x * inverse
        if low:
            normed_ref[14:16] = edge_ref[0:2, cols] * edge_scale[0:2]
        else:
            above = x_ref[0:16, cols].astype(F32)
            normed_ref[0:16] = above * wide(inverse_ref[first - 16 : first], size)
        now = normed_ref[16 : reach + 16]
        past = normed_ref[15 : reach + 15]
        older = normed_ref[14 : reach + 14]
        query, key, value = filtered(taps, now, past, older)

        convs = []
        for side, near_ref in enumerate((ahead_ref, back_ref)):
            nodal = jnp.concatenate(
                [enter_ref[i * blocks + h, PADDED * side : PADDED * (side + 1)] for h in range(blocks)], axis=1
            )
            far = jnp.dot(
                spread_ref[side * rows + first : side * rows + first + cot_ref.shape[0]],
                jnp.concatenate([nodal, nodal], axis=0),
                preferred_element_type=F32,
            )
            total = near_ref[:, cols] + far[0:reach]
            convs.append(total.astype(BF16).astype(F32))
        conv, conv_back = convs
        layer_ref[:, cols] = (x[0:count] + query[0:count] * conv[0:count]).astype(BF16)

        grads = (cot * conv, conv_back * value, conv_back * key)
        lagged = [sum(taps[j][i] * grads[j] for j in range(3)) for i in range(3)]
        one_ref[0:reach] = lagged[1]
        two_ref[0:reach] = lagged[2]
        if not low:
            one_ref[count : count + 1] = edge_ref[2:3, cols]
            two_ref[count : count + 2] = edge_ref[3:5, cols]
        scaled = lagged[0][0:count] + one_ref[1 : count + 1] + two_ref[2 : count + 2]
        base_ref[:, cols] = cot[0:count] + inverse[0:count] * scaled
        return lane_sums(scaled * x[0:count])

    def groups(i, carry):
        sums = [group(i * together + n, normed_refs.at[n], one_refs.at[n], two_refs.at[n]) for n in range(together)]
        total_ref[...] = total_ref[...] + sum(sums)
        return carry

    for p in range(pieces):
        for copy in loads[p]:
            copy.wait()
        steps = part // size // together
        lax.fori_loop(p * steps, (p + 1) * steps, groups, 0)

    mean = jnp.sum(total_ref[...], axis=1, keepdims=True) * (1.0 / width)
    scale = inverse_ref[first : first + count]
    factor = scale * scale * scale * jnp.broadcast_to(mean, (count, LANES))

    def emit(i, carry):
        cols = group_of(i)
        x = x_ref[top : top + count, cols].astype(F32)
        grad_ref[:, cols] = (base_ref[:, cols] - x * factor).astype(BF16)
        return carry

    lax.fori_loop(0, width // LANES, emit, 0, unroll=4)


def join_kernel(first, grad_ref, layer_ref, *refs):
    grad_hbm, layer_hbm, sems = refs[-3:]
    count = layer_ref.shape[0]
    half = layer_ref.shape[1] // 2
    copies = []
    for n, (source, target) in enumerate(((grad_ref, grad_hbm), (layer_ref, layer_hbm))):
        for h in range(2):
            lanes = pl.ds(h * half, half)
            copies.append(
                pltpu.make_async_copy(source.at[:, lanes], target.at[pl.ds(first, count), lanes], sems.at[n, h])
            )
    for copy in copies:
        copy.start()
    for copy in copies:
        copy.wait()


def shifted(block, axis, distance):
    devices = range(lax.axis_size(axis))
    route = [(i - distance, i) for i in devices if i - distance in devices]
    return lax.ppermute(block, axis, route)


def whole(shape):
    return pl.BlockSpec(shape, lambda *i: (0,) * len(shape))


def across(shape, step, axis=None):
    axis = len(shape) - 1 if axis is None else axis
    block = shape[:axis] + (step,) + shape[axis + 1 :]
    return pl.BlockSpec(block, lambda i: (0,) * axis + (i,) + (0,) * (len(shape) - axis - 1))


def params(mib):
    return pltpu.CompilerParams(vmem_limit_bytes=mib << 20)


def stay(array):
    return pltpu.with_memory_space_constraint(array, pltpu.HBM)


def takes(micros):
    return pl.CostEstimate(
        flops=int(micros * 1.1e9), bytes_accessed=int(micros * 3.5e6), transcendentals=0
    )


def start_call(x, cot, gain, taps, moments):
    rows, width = x.shape
    pieces = PIECES
    far = pl.BlockSpec(memory_space=pltpu.HBM)
    outs = [
        (x.shape, BF16),
        (x.shape, BF16),
        ((width // LANES, PACKET, LANES), BF16),
        ((rows, LANES), F32),
    ]
    ins = held = (x, cot, gain, taps, moments)
    return pl.pallas_call(
        start_kernel,
        in_specs=[far] * len(ins),
        out_specs=[far] * len(outs),
        out_shape=[pltpu.HBM(*out) for out in outs],
        scratch_shapes=[pltpu.VMEM(array.shape, array.dtype) for array in held]
        + [pltpu.VMEM(*out) for out in outs]
        + [
            pltpu.VMEM((min(START_TOGETHER, width // pieces // START_GROUP), rows + 8, START_GROUP), F32),
            pltpu.VMEM((2 * PADDED, width), F32),
            pltpu.SemaphoreType.DMA((pieces,)),
            pltpu.SemaphoreType.DMA((pieces,)),
            pltpu.SemaphoreType.DMA((3,)),
            pltpu.SemaphoreType.DMA((pieces,)),
            pltpu.SemaphoreType.DMA((pieces,)),
            pltpu.SemaphoreType.DMA((2,)),
        ],
        compiler_params=params(24),
        cost_estimate=takes(6),
        name="start",
    )(*[stay(array) for array in ins])


def near_call(side, signal, rates, residue, places, skip, near, mark):
    rows, width = signal.shape
    step = min(NEAR_STEP, width)
    return pl.pallas_call(
        near_kernel,
        grid=(width // step,),
        in_specs=[
            across(signal.shape, step),
            across(rates.shape, step), across(rates.shape, step), whole(places.shape),
            across(skip.shape, step),
            pl.BlockSpec((1,) + near.shape[1:], lambda i: (side, 0, 0)),
            whole((8, LANES)),
        ],
        out_specs=[across(signal.shape, step), whole((8, LANES))],
        out_shape=[pltpu.HBM(signal.shape, F32), shape((8, LANES), F32)],
        scratch_shapes=[pltpu.VMEM((NODES * rows, min(NEAR_GROUP, width)), BF16)],
        compiler_params=params(16),
        cost_estimate=takes(4),
        name="near",
    )(stay(signal), rates, residue, places, skip, stay(near), mark)


def scan_call(rates, residue, skip, gain, taps, places, gathered, mark, rows):
    count = gathered.shape[0]
    return pl.pallas_call(
        functools.partial(scan_kernel, rows=rows, nodes=[float(p) for p in node_places(rows)]),
        out_shape=[shape(gathered.shape, BF16), shape((8, LANES), F32)],
        scratch_shapes=[
            pltpu.VMEM((count * PACKET, LANES), F32),
            pltpu.VMEM((8, count, LANES), F32),
            pltpu.VMEM((4, count, LANES), F32),
            pltpu.VMEM((MODES, PADDED, LANES), F32),
            pltpu.VMEM((NODES, MODES, LANES), F32),
        ],
        compiler_params=params(8),
        cost_estimate=takes(2),
        name="scan",
    )(rates, residue, skip, gain, taps, places, gathered, mark)


def finish_call(rows, first, count, *arrays):
    x = arrays[0]
    width = x.shape[1]
    low = first == 0
    pieces = PIECES
    size = min(FINISH_GROUP, width)
    together = min(FINISH_TOGETHER, width // pieces // size)
    far = pl.BlockSpec(memory_space=pltpu.HBM)
    near = pl.BlockSpec(memory_space=pltpu.VMEM)
    half = shape((count, width), BF16)
    out_shape = [half, half]
    above, below, reach = (0, 16, count + 8) if low else (16, 0, count)
    if low:
        out_shape += [shape((16, width), F32)]
    return pl.pallas_call(
        functools.partial(finish_kernel, rows, first, count),
        in_specs=[far] * 4 + [near] * (len(arrays) - 4),
        out_specs=[near] * len(out_shape),
        out_shape=out_shape,
        scratch_shapes=[
            pltpu.VMEM((above + count + below, width), BF16),
            pltpu.VMEM((count + below, width), BF16),
            pltpu.VMEM((reach, width), F32),
            pltpu.VMEM((reach, width), F32),
            pltpu.VMEM((count, width), F32),
            pltpu.VMEM((together, reach + 24, size), F32),
            pltpu.VMEM((together, reach + 8, size), F32),
            pltpu.VMEM((together, reach + 8, size), F32),
            pltpu.VMEM((count, LANES), F32),
            pltpu.SemaphoreType.DMA((4, pieces)),
        ],
        compiler_params=params(24),
        cost_estimate=takes(6),
        name="finish",
    )(*[stay(array) for array in arrays[:4]], *arrays[4:])


def join_call(rows, first, grad, layer, *wholes):
    far = pl.BlockSpec(memory_space=pltpu.HBM)
    near = pl.BlockSpec(memory_space=pltpu.VMEM)
    out = shape((rows, layer.shape[1]), BF16)
    return pl.pallas_call(
        functools.partial(join_kernel, first),
        in_specs=[near, near] + [far] * len(wholes),
        out_specs=[far, far],
        out_shape=[out, out],
        scratch_shapes=[pltpu.SemaphoreType.DMA((2, 2))],
        input_output_aliases={2 + n: n for n in range(len(wholes))},
        compiler_params=params(4),
        cost_estimate=takes(1),
        name="join",
    )(grad, layer, *wholes)


def local(section_input, cotangent, norm_gain, short_filter, decay_rate, residue, skip_gain):
    x = section_input[0]
    cot = cotangent[0]
    rows = x.shape[0]
    taps = jnp.transpose(short_filter, (1, 2, 0, 3))
    rates = decay_rate[0]
    fixed = {name: jnp.asarray(table) for name, table in constants(rows).items()}

    weights = residue[0]
    mixed, gate, packet, inverse = start_call(x, cot, norm_gain, taps, fixed["moments"])
    gathered = lax.all_to_all(packet, "seq", split_axis=0, concat_axis=0, tiled=True)
    near = (rates, weights, fixed["places"], skip_gain, fixed["near"])
    ahead, mark = near_call(0, mixed, *near, stay(inverse))
    entering, mark = scan_call(rates, weights, skip_gain, norm_gain, taps, fixed["places"], gathered, mark, rows)
    enter = lax.all_to_all(entering, "seq", split_axis=0, concat_axis=0, tiled=True)
    back, mark = near_call(1, gate, *near, mark)

    common = (x, cot, ahead, back, inverse, norm_gain, taps, fixed["spread"], enter)
    grad, layer, edge = finish_call(rows, 0, SPLIT, *common)
    back_low = shifted(grad, "section", -1)
    on_low = shifted(layer, "section", 1)
    grad, layer = finish_call(rows, SPLIT, rows - SPLIT, *common, edge)
    back_high = shifted(grad, "section", -1)
    on_high = shifted(layer, "section", 1)
    joined = join_call(rows, 0, back_low, on_low)
    passed_back, passed_on = join_call(rows, SPLIT, back_high, on_high, *joined)
    return passed_on[None], passed_back[None]


def solution(mesh):
    in_specs = (
        P("section", "seq", None),
        P("section", "seq", None),
        P("section", None),
        P("section", None, None, None),
        P("section", None, None),
        P("section", None, None),
        P("section", None),
    )
    out_specs = (P("section", "seq", None), P("section", "seq", None))
    return jax.shard_map(local, mesh=mesh, in_specs=in_specs, out_specs=out_specs, check_vma=False)
```
